256 devices in a mesh: grp: 2 (over core), img: 16 (over x_hi, z), tp: 8 (over x_lo, y).
Axes of the slice: x: 4 (x_hi: 2, x_lo: 2; x = x_hi * 2 + x_lo), y: 4, z: 8, core: 2. Of those that a mesh axis runs over, the one named last changes fastest.
Arguments:
- features: bfloat16 [2, 8192, 256], P('grp', 'img'), may hold values from -7 to 7
- masters: float32 [2, 65536, 256], P('grp', ('img', 'tp')), may hold values from -7 to 7
- patch_mask: int32 [8192], P('img'), may hold values from 0 to 1, as said below
Outputs:
- updated: float32 [2, 65536, 256], P('grp', ('img', 'tp'))
The draws below stay inside these ranges and needn't reach their ends.
Inputs may be any that keep to these rules, and one draw needn't show every extreme that they name: `patch_mask`: 1 marks a masked student patch; some crops have no masked patch.
All inputs are finite; a program needn't handle non-finite values.
Results may differ from the reference program's by a relative error of at most 0.0045.
Values may be sent and summed in bfloat16 or wider, within the bound.
No kernel may reach another device: no remote copies, remote signals or barrier semaphores. Data moves between devices by JAX's collectives and lax.ppermute only.
A program may use at most 128 MiB of HBM per device.

```python
import jax
import jax.numpy as jnp
from jax import lax

K = 256
PROTOS = 65536
PATCHES = 256
BALANCE_STEPS = 3
TOKENS = 8192
N_IMG = 16
N_TP = 8


def shared_direction(key):
    bits = jax.random.randint(jax.random.fold_in(key, 101), (K,), 0, 2)
    return (2 * bits - 1).astype(jnp.float32)


def row_level(key):
    order = jax.random.permutation(jax.random.fold_in(key, 103), N_IMG)
    centre = 2.0 * order.astype(jnp.float32) / max(N_IMG - 1, 1) - 1.0
    jitter = jax.random.uniform(jax.random.fold_in(key, 107), (TOKENS,), jnp.float32, -0.45, 0.45)
    shard = (jnp.arange(TOKENS) // (TOKENS // N_IMG)).astype(jnp.int32)
    return jnp.clip(0.6 * centre[shard] + jitter, -1.0, 1.0)


def proto_level(key):
    shard_rows = PROTOS // (N_IMG * N_TP)
    tp_place = (jnp.arange(PROTOS) // shard_rows % N_TP).astype(jnp.int32)
    tilt = 2.0 * tp_place.astype(jnp.float32) / max(N_TP - 1, 1) - 1.0
    spread = jax.random.uniform(jax.random.fold_in(key, 109), (PROTOS,), jnp.float32, -0.6, 0.6)
    return jnp.clip(0.4 * tilt + spread, -1.0, 1.0)


def draw_features(key, part):
    signs = shared_direction(key)
    level = row_level(key)
    key = jax.random.fold_in(key, 5)
    noise = jnp.clip(jax.random.normal(key, (2, TOKENS, K), jnp.float32), -6.0, 6.0)
    reach = 1.3
    values = noise + reach * level[None, :, None] * signs[None, None, :]
    return jnp.clip(values, -7.0, 7.0).astype(jnp.bfloat16)


def draw_masters(key, part):
    signs = shared_direction(key)
    level = proto_level(key)
    key = jax.random.fold_in(key, 11)
    noise = jnp.clip(jax.random.normal(key, (2, PROTOS, K), jnp.float32), -6.0, 6.0)
    reach = 2.5
    values = noise + reach * level[None, :, None] * signs[None, None, :]
    return jnp.clip(values, -7.0, 7.0)


def draw_patch_mask(key, part):
    key = jax.random.fold_in(key, 7)
    mask_key, key_limit, key_roll = jax.random.split(key, 3)
    crop_count = TOKENS // PATCHES
    flagged = jax.random.randint(mask_key, (crop_count, 1), 0, 2)
    limit = jax.random.randint(key_limit, (crop_count, 1), 100, 501)
    rolled = jax.random.randint(key_roll, (crop_count, PATCHES), 0, 1000)
    return (flagged * (rolled < limit).astype(jnp.int32)).astype(jnp.int32).reshape(TOKENS)


def setup_inputs(seed: int = 0) -> dict:
    seeds = jax.random.split(jax.random.key(seed), 4)
    return {
        "features": draw_features(jax.random.fold_in(seeds[3], 71), 0),
        "masters": draw_masters(jax.random.fold_in(seeds[3], 71), 0),
        "patch_mask": draw_patch_mask(jax.random.fold_in(seeds[3], 71), 0),
    }


MOMENTUM = 0.994
TEACHER_TEMP = 0.07
STUDENT_TEMP = 0.1
EPS = 1e-06

def unit_rows(values):
    values = values.astype(jnp.float32)
    return (values / jnp.sqrt(lax.optimization_barrier(jnp.sum(values * values, -1, keepdims=True)) + EPS)).astype(jnp.bfloat16)

def exp_block(token_batch, proto_block, inverse_temp):
    return jnp.exp(jnp.dot(token_batch, proto_block.T, preferred_element_type=jnp.float32) * inverse_temp)

def reference(features, masters, patch_mask):
    blended = MOMENTUM * masters[1] + (1.0 - MOMENTUM) * masters[0]
    student_protos = unit_rows(masters[0])
    teacher_protos = unit_rows(blended)
    student_tokens = unit_rows(features[0])
    teacher_tokens = unit_rows(features[1])
    masked = patch_mask.astype(jnp.float32).reshape(-1, PATCHES)
    counts = lax.optimization_barrier(jnp.sum(masked, 1, keepdims=True))
    row_weight = (masked / (STUDENT_TEMP * jnp.maximum(counts, 1.0))).reshape(-1).astype(jnp.bfloat16)
    row_weight = lax.optimization_barrier(row_weight).astype(jnp.float32)
    block_count = 16
    block_size = PROTOS // block_count
    teacher_blocks = teacher_protos.reshape(block_count, block_size, K)
    student_blocks = student_protos.reshape(block_count, block_size, K)
    row_scale = jnp.ones((TOKENS,), jnp.float32)
    col_scale = jnp.ones((block_count, block_size), jnp.float32)
    row_sum = jnp.ones((TOKENS,), jnp.float32)
    for balance_sweep in range(BALANCE_STEPS):

        def column(proto_block):
            return jnp.dot(row_scale, exp_block(teacher_tokens, proto_block, 1.0 / TEACHER_TEMP), precision=lax.Precision.HIGHEST)
        col_scale = 1.0 / lax.map(column, teacher_blocks)

        def accumulate(running, input_arrays):
            proto_block, scale_block = input_arrays
            term = jnp.dot(exp_block(teacher_tokens, proto_block, 1.0 / TEACHER_TEMP), scale_block, precision=lax.Precision.HIGHEST)
            return (running + term, None)
        row_sum, unused = lax.scan(accumulate, jnp.zeros((TOKENS,), jnp.float32), (teacher_blocks, col_scale))
        row_scale = 1.0 / row_sum

    def student_sum(running, proto_block):
        return (running + lax.optimization_barrier(jnp.sum(exp_block(student_tokens, proto_block, 1.0 / STUDENT_TEMP), 1)), None)
    student_total, unused = lax.scan(student_sum, jnp.zeros((TOKENS,), jnp.float32), student_blocks)

    def loss_gradient(input_arrays):
        teacher_block, student_block, scale_block = input_arrays
        targets = (exp_block(teacher_tokens, teacher_block, 1.0 / TEACHER_TEMP) * scale_block[None, :] / row_sum[:, None]).astype(jnp.bfloat16)
        targets = lax.optimization_barrier(targets).astype(jnp.float32)
        probs = exp_block(student_tokens, student_block, 1.0 / STUDENT_TEMP) / student_total[:, None]
        error_rows = (PROTOS * (probs - targets) * row_weight[:, None]).astype(jnp.bfloat16)
        return jnp.einsum('rp,rk->pk', error_rows, student_tokens, preferred_element_type=jnp.float32)
    grads = lax.map(loss_gradient, (teacher_blocks, student_blocks, col_scale)).reshape(PROTOS, K)
    return jnp.stack([grads, blended])
```

```python
import functools

import jax
import jax.numpy as jnp
from jax import lax
from jax.experimental import pallas as pl
from jax.experimental.pallas import tpu as pltpu
from jax.sharding import PartitionSpec as P

PROTOS = 65536
PATCHES = 256
MOMENTUM = 0.994
TEACHER_TEMP = 0.07
STUDENT_TEMP = 0.1
EPS = 1e-06

AXES = ("grp", "img", "tp")
N_GRP, N_IMG, N_TP = 2, 16, 8
N_Y = 4
HALF = 256
OWN_ROWS = 64
ROWS = N_IMG * OWN_ROWS
OWN = N_Y * HALF
COLS = 2 * OWN
N_ROWGRP = 32
N_COLGRP = 8
VMEM_LIMIT = 40 * 1024 * 1024


def coordinates(device):
    grp, rest = divmod(device, N_IMG * N_TP)
    img, tp = divmod(rest, N_TP)
    x_lo, y = divmod(tp, N_Y)
    return grp, img, x_lo, y


def groups_of(key):
    found = {}
    for device in range(N_GRP * N_IMG * N_TP):
        found.setdefault(key(*coordinates(device)), []).append(device)
    return list(found.values())


Y_GROUPS = groups_of(lambda grp, img, x_lo, y: (grp, img, x_lo))
COL_GROUPS = groups_of(lambda grp, img, x_lo, y: (img, x_lo))
ROW_GROUPS = groups_of(lambda grp, img, x_lo, y: (grp, y))


def exchange(blocks, groups):
    return lax.all_to_all(blocks, AXES, 0, 0, axis_index_groups=groups, tiled=True)


def swapped(block):
    return lax.ppermute(block, "grp", [(0, 1), (1, 0)])


def unit_rows(values):
    values = values.astype(jnp.float32)
    return (values / jnp.sqrt(jnp.sum(values * values, -1, keepdims=True) + EPS)).astype(
        jnp.bfloat16
    )


def diagonal():
    return lax.broadcasted_iota(jnp.int32, (128, 128), 0) == lax.broadcasted_iota(
        jnp.int32, (128, 128), 1
    )


def to_row(column):
    return jnp.sum(jnp.where(diagonal(), column, 0.0), axis=0, keepdims=True)


def to_column(row):
    return jnp.sum(jnp.where(diagonal(), row, 0.0), axis=1, keepdims=True)


def lanes(pieces):
    return jnp.concatenate([pieces[k : k + 1, :] for k in range(pieces.shape[0])], axis=1)


def pieces_of(row):
    return jnp.concatenate([row[:, k * 128 : (k + 1) * 128] for k in range(8)], axis=0)


def send_columns(grp_ref, vector_ref, out_ref):
    top, bottom = vector_ref[0:8, :], vector_ref[8:16, :]
    for target in range(2):
        same = grp_ref[0] == target
        first = jnp.where(same, top, bottom)
        second = jnp.where(same, bottom, top)
        for y in range(N_Y):
            out_ref[target * N_Y + y, 0:8, :] = first
            out_ref[target * N_Y + y, 8:16, :] = second


def teacher_exp_kernel(grp_ref, own_ref, other_ref, token_ref, exp_ref, out_ref, vector_ref):
    for part, proto_ref in enumerate((own_ref, other_ref)):

        @pl.loop(0, OWN // 256)
        def _(i):
            protos = proto_ref[pl.ds(i * 256, 256), :]
            logits = lax.dot_general(
                protos,
                token_ref[...],
                (((1,), (1,)), ((), ())),
                preferred_element_type=jnp.float32,
            )
            values = jnp.exp(logits * (1.0 / TEACHER_TEMP))
            exp_ref[pl.ds(part * OWN + i * 256, 256), :] = values
            folded = sum(values[:, k * 128 : (k + 1) * 128] for k in range(8))
            column = jnp.sum(folded, axis=1, keepdims=True)
            for h in range(2):
                vector_ref[pl.ds(part * 8 + i * 2 + h, 1), :] = to_row(
                    column[h * 128 : (h + 1) * 128]
                )

    send_columns(grp_ref, vector_ref, out_ref)


def student_exp_kernel(own_ref, other_ref, token_ref, exp_ref, out_ref, total_ref):
    total_ref[...] = jnp.zeros_like(total_ref)
    for part, proto_ref in enumerate((own_ref, other_ref)):

        @pl.loop(0, OWN // 256)
        def _(i):
            protos = proto_ref[pl.ds(i * 256, 256), :]
            logits = lax.dot_general(
                protos,
                token_ref[...],
                (((1,), (1,)), ((), ())),
                preferred_element_type=jnp.float32,
            )
            values = jnp.exp(logits * (1.0 / STUDENT_TEMP))
            exp_ref[pl.ds(part * OWN + i * 256, 256), :] = values
            total_ref[...] += jnp.sum(values.reshape(32, 8, ROWS), axis=0)

    out_ref[...] = pieces_of(jnp.sum(total_ref[...], axis=0, keepdims=True))


def row_kernel(with_student, *refs):
    if with_student:
        parts_ref, exp_ref, student_ref, out_ref, scale_ref, total_ref = refs
    else:
        parts_ref, exp_ref, out_ref, scale_ref, total_ref = refs
    scale_ref[...] = 1.0 / jnp.sum(parts_ref[...], axis=0)
    total_ref[...] = jnp.zeros_like(total_ref)

    @pl.loop(0, COLS // 128)
    def _(j):
        column = to_column(scale_ref[pl.ds(j, 1), :])
        weighted = exp_ref[pl.ds(j * 128, 128), :] * column
        total_ref[...] += jnp.sum(weighted.reshape(16, 8, ROWS), axis=0)

    mine = pieces_of(jnp.sum(total_ref[...], axis=0, keepdims=True))
    for k in range(N_ROWGRP):
        out_ref[k, 0:8, :] = mine
        if with_student:
            out_ref[k, 8:16, :] = student_ref[...]


def col_kernel(with_student, *refs):
    if with_student:
        grp_ref, parts_ref, exp_ref, out_ref, student_ref, vector_ref = refs
    else:
        grp_ref, parts_ref, exp_ref, out_ref, vector_ref = refs
    total = jnp.sum(parts_ref[...], axis=0)
    inverse = 1.0 / total
    row = lanes(inverse[0:8, :])
    if with_student:
        student_ref[...] = inverse[8:16, :]

    @pl.loop(0, COLS // 128)
    def _(j):
        weighted = exp_ref[pl.ds(j * 128, 128), :] * row
        folded = sum(weighted[:, k * 128 : (k + 1) * 128] for k in range(8))
        vector_ref[pl.ds(j, 1), :] = to_row(jnp.sum(folded, axis=1, keepdims=True))

    send_columns(grp_ref, vector_ref, out_ref)


def grad_kernel(
    parts_ref,
    scale_ref,
    student_ref,
    weight_ref,
    teacher_exp_ref,
    student_exp_ref,
    token_ref,
    own_ref,
    other_ref,
):
    row_inverse = lanes(1.0 / jnp.sum(parts_ref[...], axis=0))
    student_inverse = lanes(student_ref[...])
    weight = lanes(weight_ref[...])

    for part, out_ref in enumerate((own_ref, other_ref)):

        @pl.loop(0, OWN // 256)
        def _(i):
            errors = []
            for h in range(2):
                j = part * 8 + i * 2 + h
                column = to_column(scale_ref[pl.ds(j, 1), :])
                rows = pl.ds(j * 128, 128)
                targets = (teacher_exp_ref[rows, :] * column * row_inverse).astype(jnp.bfloat16)
                probs = student_exp_ref[rows, :] * student_inverse
                errors.append(
                    (PROTOS * (probs - targets.astype(jnp.float32)) * weight).astype(jnp.bfloat16)
                )
            out_ref[pl.ds(i * 256, 256), :] = jnp.dot(
                jnp.concatenate(errors, axis=0),
                token_ref[...],
                preferred_element_type=jnp.float32,
            ).astype(out_ref.dtype)


def call(kernel, outs, scratch, *args, flops=0, transcendentals=0):
    vmem = pl.BlockSpec(memory_space=pltpu.VMEM)
    smem = pl.BlockSpec(memory_space=pltpu.SMEM)
    return pl.pallas_call(
        kernel,
        out_shape=outs,
        in_specs=[smem if a.dtype == jnp.int32 else vmem for a in args],
        out_specs=[vmem] * len(outs),
        scratch_shapes=scratch,
        compiler_params=pltpu.CompilerParams(vmem_limit_bytes=VMEM_LIMIT),
        cost_estimate=pl.CostEstimate(
            flops=flops, transcendentals=transcendentals, bytes_accessed=COLS * ROWS * 4
        ),
    )(*args)


def shape(dims, dtype=jnp.float32):
    return jax.ShapeDtypeStruct(dims, dtype)


def per_device(features, masters, patch_mask):
    grp = lax.axis_index("grp")
    y = lax.axis_index("tp") % N_Y
    teacher = grp == 1
    grp_word = grp.astype(jnp.int32).reshape(1)
    vec = pltpu.VMEM((16, 128), jnp.float32)
    wide = pltpu.VMEM((8, ROWS), jnp.float32)

    own_master = masters[0]
    other_master = swapped(own_master)
    start = y * (2 * OWN_ROWS)
    own_rows = lax.dynamic_slice_in_dim(features[0], start + grp * OWN_ROWS, OWN_ROWS)
    lent_rows = lax.dynamic_slice_in_dim(features[0], start + (1 - grp) * OWN_ROWS, OWN_ROWS)
    other_rows = swapped(lent_rows)

    student_master = jnp.where(teacher, other_master, own_master)
    teacher_master = jnp.where(teacher, own_master, other_master)
    blended = MOMENTUM * teacher_master + (1.0 - MOMENTUM) * student_master
    teacher_half = unit_rows(lax.dynamic_slice_in_dim(blended, grp * HALF, HALF))
    student_half = unit_rows(lax.dynamic_slice_in_dim(student_master, grp * HALF, HALF))
    teacher_rows = unit_rows(jnp.where(teacher, own_rows, other_rows))
    student_rows = unit_rows(jnp.where(teacher, other_rows, own_rows))

    masked = patch_mask.astype(jnp.float32).reshape(-1, PATCHES)
    counts = jnp.sum(masked, 1, keepdims=True)
    row_weight = (
        (masked / (STUDENT_TEMP * jnp.maximum(counts, 1.0))).reshape(-1).astype(jnp.bfloat16)
    )
    own_weight = lax.dynamic_slice_in_dim(row_weight, start + grp * OWN_ROWS, OWN_ROWS)
    student_pack = jnp.concatenate(
        [student_rows, jnp.pad(own_weight.reshape(1, OWN_ROWS), ((0, 15), (0, 256 - OWN_ROWS)))]
    )

    teacher_own = exchange(
        jnp.broadcast_to(teacher_half[None], (N_Y, HALF, 256)), Y_GROUPS
    ).reshape(OWN, 256)
    teacher_other = swapped(teacher_own)
    teacher_tokens = lax.all_to_all(
        jnp.broadcast_to(teacher_rows[None], (N_IMG, OWN_ROWS, 256)), "img", 0, 0, tiled=True
    ).reshape(ROWS, 256)

    student_own = lax.all_gather(
        student_half, AXES, axis_index_groups=Y_GROUPS, axis=0, tiled=True
    )
    student_other = swapped(student_own)
    packs = lax.all_gather(student_pack, "img", axis=0)
    student_tokens = packs[:, :OWN_ROWS].reshape(ROWS, 256)
    weights = packs[:, OWN_ROWS, :OWN_ROWS].astype(jnp.float32).reshape(8, 128)

    work = COLS * ROWS
    teacher_exp, col_parts = call(
        teacher_exp_kernel,
        [shape((COLS, ROWS)), shape((N_COLGRP, 16, 128))],
        [vec],
        grp_word,
        teacher_own,
        teacher_other,
        teacher_tokens,
        flops=2 * work * 256,
        transcendentals=work,
    )
    student_exp, student_part = call(
        student_exp_kernel,
        [shape((COLS, ROWS)), shape((8, 128))],
        [wide],
        student_own,
        student_other,
        student_tokens,
        flops=2 * work * 256,
        transcendentals=work,
    )

    for sweep in range(3):
        last = sweep == 2
        col_parts = exchange(col_parts, COL_GROUPS)
        row_parts, col_scale = call(
            functools.partial(row_kernel, sweep == 1),
            [shape((N_ROWGRP, 16 if sweep == 1 else 8, 128)), shape((16, 128))],
            [wide],
            col_parts,
            teacher_exp,
            *((student_part,) if sweep == 1 else ()),
            flops=2 * work,
        )
        row_parts = exchange(row_parts, ROW_GROUPS)
        if not last:
            results = call(
                functools.partial(col_kernel, sweep == 1),
                [shape((N_COLGRP, 16, 128))] + ([shape((8, 128))] if sweep == 1 else []),
                [vec],
                grp_word,
                row_parts,
                teacher_exp,
                flops=2 * work,
            )
            col_parts = results[0]
            if sweep == 1:
                student_inverse = results[1]

    own_grad, other_grad = call(
        grad_kernel,
        [shape((OWN, 256)), shape((OWN, 256), jnp.bfloat16)],
        [],
        row_parts,
        col_scale,
        student_inverse,
        weights,
        teacher_exp,
        student_exp,
        student_tokens,
        flops=2 * work * 256,
    )
    chip_grad = own_grad + swapped(other_grad).astype(jnp.float32)
    received = exchange(chip_grad.astype(jnp.bfloat16).reshape(N_Y, HALF, 256), Y_GROUPS)
    half_grad = jnp.sum(received.astype(jnp.float32), axis=0)
    second = lax.ppermute(half_grad, "grp", [(1, 0)])
    gradient = jnp.concatenate([half_grad, second])
    return jnp.where(teacher, blended, gradient)[None]


def solution(mesh):
    in_specs = (P("grp", "img", None), P("grp", ("img", "tp"), None), P("img"))
    out_specs = P("grp", ("img", "tp"), None)
    return jax.shard_map(
        per_device, mesh=mesh, in_specs=in_specs, out_specs=out_specs, check_vma=False
    )
```

```python
import functools

import jax
import jax.numpy as jnp
from jax import lax
from jax.experimental import pallas as pl
from jax.experimental.pallas import tpu as pltpu
from jax.sharding import PartitionSpec as P

PROTOS = 65536
PATCHES = 256
MOMENTUM = 0.994
TEACHER_TEMP = 0.07
STUDENT_TEMP = 0.1
EPS = 1e-06

AXES = ("grp", "img", "tp")
N_GRP, N_IMG, N_TP = 2, 16, 8
N_Y = 4
BLOCK = 512
OWN_ROWS = 64
PACK = 2 * OWN_ROWS + 16
ROWS = N_IMG * OWN_ROWS
COLS = N_Y * BLOCK
N_ROWGRP = 32
N_COLGRP = 8
VMEM_LIMIT = 16 * 1024 * 1024


def coordinates(device):
    grp, rest = divmod(device, N_IMG * N_TP)
    img, tp = divmod(rest, N_TP)
    x_lo, y = divmod(tp, N_Y)
    return grp, img, x_lo, y


def groups_of(key):
    found = {}
    for device in range(N_GRP * N_IMG * N_TP):
        found.setdefault(key(*coordinates(device)), []).append(device)
    return list(found.values())


COL_GROUPS = groups_of(lambda grp, img, x_lo, y: (img, x_lo))
ROW_GROUPS = groups_of(lambda grp, img, x_lo, y: (grp, y))


def exchange(blocks, groups):
    return lax.all_to_all(blocks, AXES, 0, 0, axis_index_groups=groups, tiled=True)


def swapped(block):
    return lax.ppermute(block, "grp", [(0, 1), (1, 0)])


def from_y(block, distance, only_student=False):
    route = []
    for grp in range(1 if only_student else N_GRP):
        for rest in range(N_IMG * N_TP):
            base = grp * N_IMG * N_TP + rest // N_Y * N_Y
            y = rest % N_Y
            route.append((base + (y + distance) % N_Y, base + y))
    return lax.ppermute(block, AXES, route)


def unit_rows(values):
    return (values / jnp.sqrt(jnp.sum(values * values, -1, keepdims=True) + EPS)).astype(
        jnp.bfloat16
    )


def diagonal():
    return lax.broadcasted_iota(jnp.int32, (128, 128), 0) == lax.broadcasted_iota(
        jnp.int32, (128, 128), 1
    )


def to_row(column):
    return jnp.sum(jnp.where(diagonal(), column, 0.0), axis=0, keepdims=True)


def to_column(row):
    return jnp.sum(jnp.where(diagonal(), row, 0.0), axis=1, keepdims=True)


def lanes(pieces):
    return jnp.concatenate([pieces[k : k + 1, :] for k in range(pieces.shape[0])], axis=1)


def pieces_of(row):
    return jnp.concatenate([row[:, k * 128 : (k + 1) * 128] for k in range(8)], axis=0)


def token_kernel(place_ref, features_ref, other_ref, mask_ref, out_ref):
    grp, y = place_ref[0], place_ref[1]
    start = pl.multiple_of(y * (2 * OWN_ROWS) + grp * OWN_ROWS, OWN_ROWS)
    own = unit_rows(features_ref[pl.ds(start, OWN_ROWS), :].astype(jnp.float32))
    other = unit_rows(other_ref[...].astype(jnp.float32))
    student = jnp.where(grp == 0, own, other)
    teacher = jnp.where(grp == 0, other, own)
    crop = mask_ref[pl.ds(y // 2 * 2, 2), :].astype(jnp.float32)
    count = jnp.maximum(jnp.sum(crop), 1.0)
    weight = mask_ref[pl.ds(y, 1), :].astype(jnp.float32) / (STUDENT_TEMP * count)
    weight = jnp.where(grp == 0, weight, pltpu.roll(weight, 64, 1))
    weight = jnp.broadcast_to(jnp.concatenate([weight, weight], axis=1), (16, 256))
    weight = weight.astype(jnp.bfloat16)
    for k in range(N_IMG):
        out_ref[k, 0:OWN_ROWS, :] = teacher
        out_ref[k, OWN_ROWS : 2 * OWN_ROWS, :] = student
        out_ref[k, 2 * OWN_ROWS : PACK, :] = weight


def proto_kernel(place_ref, own_ref, other_ref, master_ref, unit_ref):
    own = own_ref[...]
    blended = MOMENTUM * own + (1.0 - MOMENTUM) * other_ref[...]
    master = jnp.where(place_ref[0] == 1, blended, own)
    master_ref[...] = master
    unit_ref[...] = unit_rows(master)


def exp_kernel(*refs):
    place_ref, pack_ref = refs[:2]
    own_refs, other_refs = refs[2:6], refs[6:10]
    teacher_ref, student_ref, parts_ref, total_ref, token_ref, weight_ref = refs[10:16]
    scratch_ref, vector_ref, wide_ref = refs[16:]
    grp, y = place_ref[0], place_ref[1]
    left = lax.broadcasted_iota(jnp.int32, (1, 128), 1) < OWN_ROWS
    for k in range(N_IMG):
        rows = slice(k * OWN_ROWS, (k + 1) * OWN_ROWS)
        scratch_ref[rows, :] = pack_ref[k, 0:OWN_ROWS, :]
        token_ref[rows, :] = pack_ref[k, OWN_ROWS : 2 * OWN_ROWS, :]
    for k in range(N_IMG // 2):
        first, second = (
            pack_ref[2 * k + j, 2 * OWN_ROWS : PACK, 0:128].astype(jnp.float32)[0:1, :]
            for j in range(2)
        )
        weight_ref[k : k + 1, :] = jnp.where(left, first, pltpu.roll(second, 64, 1))

    def logits_of(protos, tokens):
        return lax.dot_general(
            protos, tokens, (((1,), (1,)), ((), ())), preferred_element_type=jnp.float32
        )

    wide_ref[...] = jnp.zeros_like(wide_ref)
    for k in range(N_Y):
        base = (y + k) % N_Y * BLOCK

        @pl.loop(0, BLOCK // 256)
        def _(i):
            own = own_refs[k][pl.ds(i * 256, 256), :]
            other = other_refs[k][pl.ds(i * 256, 256), :]
            student = jnp.where(grp == 0, own, other)
            teacher = jnp.where(grp == 0, other, own)
            rows = pl.ds(pl.multiple_of(base + i * 256, 256), 256)

            values = jnp.exp(logits_of(teacher, scratch_ref[...]) * (1.0 / TEACHER_TEMP))
            teacher_ref[rows, :] = values
            folded = sum(values[:, k * 128 : (k + 1) * 128] for k in range(8))
            column = jnp.sum(folded, axis=1, keepdims=True)
            for h in range(2):
                vector_ref[pl.ds(base // 128 + i * 2 + h, 1), :] = to_row(
                    column[h * 128 : (h + 1) * 128]
                )

            values = jnp.exp(logits_of(student, token_ref[...]) * (1.0 / STUDENT_TEMP))
            student_ref[rows, :] = values
            wide_ref[...] += jnp.sum(values.reshape(32, 8, ROWS), axis=0)

    total_ref[...] = pieces_of(jnp.sum(wide_ref[...], axis=0, keepdims=True))
    for k in range(N_COLGRP):
        parts_ref[k] = vector_ref[...]


def row_kernel(with_student, *refs):
    if with_student:
        parts_ref, exp_ref, student_ref, out_ref, scale_ref = refs
    else:
        parts_ref, exp_ref, out_ref, scale_ref = refs
    scale = 1.0 / jnp.sum(parts_ref[...], axis=0)
    scale_ref[...] = scale
    total = jnp.zeros((8, ROWS), jnp.float32)
    for j in range(COLS // 128):
        weighted = exp_ref[j * 128 : (j + 1) * 128, :] * to_column(scale[j : j + 1, :])
        total += jnp.sum(weighted.reshape(16, 8, ROWS), axis=0)
    mine = pieces_of(jnp.sum(total, axis=0, keepdims=True))
    for k in range(N_ROWGRP):
        out_ref[k, 0:8, :] = mine
        if with_student:
            out_ref[k, 8:16, :] = student_ref[...]


def col_kernel(with_student, *refs):
    if with_student:
        parts_ref, exp_ref, out_ref, student_ref, vector_ref = refs
    else:
        parts_ref, exp_ref, out_ref, vector_ref = refs
    inverse = 1.0 / jnp.sum(parts_ref[...], axis=0)
    row = lanes(inverse[0:8, :])
    if with_student:
        student_ref[...] = inverse[8:16, :]
    for j in range(COLS // 128):
        weighted = exp_ref[j * 128 : (j + 1) * 128, :] * row
        folded = sum(weighted[:, k * 128 : (k + 1) * 128] for k in range(8))
        vector_ref[j : j + 1, :] = to_row(jnp.sum(folded, axis=1, keepdims=True))
    for k in range(N_COLGRP):
        out_ref[k] = vector_ref[...]


def grad_kernel(
    parts_ref,
    scale_ref,
    student_ref,
    weight_ref,
    teacher_exp_ref,
    student_exp_ref,
    token_ref,
    own_ref,
    sent_ref,
):
    row_inverse = lanes(1.0 / jnp.sum(parts_ref[...], axis=0))
    student_inverse = lanes(student_ref[...])
    weight = lanes(weight_ref[...])

    @pl.loop(0, COLS // 256)
    def _(i):
        errors = []
        for h in range(2):
            j = i * 2 + h
            column = to_column(scale_ref[pl.ds(j, 1), :])
            rows = pl.ds(j * 128, 128)
            targets = (teacher_exp_ref[rows, :] * column * row_inverse).astype(jnp.bfloat16)
            probs = student_exp_ref[rows, :] * student_inverse
            errors.append(
                (PROTOS * (probs - targets.astype(jnp.float32)) * weight).astype(jnp.bfloat16)
            )
        gradient = jnp.dot(
            jnp.concatenate(errors, axis=0), token_ref[...], preferred_element_type=jnp.float32
        )
        own_ref[pl.ds(i * 256, 256), :] = gradient
        sent_ref[pl.ds(i * 256, 256), :] = gradient.astype(jnp.bfloat16)


def split_kernel(place_ref, own_ref, received_ref, mine_ref, *out_refs):
    y = place_ref[1]
    for k in range(N_Y):
        rows = pl.ds(pl.multiple_of((y + k) % N_Y * BLOCK, BLOCK), BLOCK)
        block = own_ref[rows, :] + received_ref[rows, :].astype(jnp.float32)
        if k == 0:
            mine_ref[...] = block
        else:
            out_refs[k - 1][...] = block.astype(jnp.bfloat16)


def call(kernel, outs, scratch, *args, flops=0, transcendentals=0):
    vmem = pl.BlockSpec(memory_space=pltpu.VMEM)
    smem = pl.BlockSpec(memory_space=pltpu.SMEM)
    return pl.pallas_call(
        kernel,
        out_shape=outs,
        in_specs=[smem if a.ndim == 1 else vmem for a in args],
        out_specs=[vmem] * len(outs),
        scratch_shapes=scratch,
        compiler_params=pltpu.CompilerParams(vmem_limit_bytes=VMEM_LIMIT),
        cost_estimate=pl.CostEstimate(
            flops=flops, transcendentals=transcendentals, bytes_accessed=COLS * ROWS * 4
        ),
    )(*args)


def shape(dims, dtype=jnp.float32):
    return jax.ShapeDtypeStruct(dims, dtype)


def per_device(features, masters, patch_mask):
    grp = lax.axis_index("grp")
    y = lax.axis_index("tp") % N_Y
    teacher = grp == 1
    place = jnp.stack([grp, y]).astype(jnp.int32)
    work = COLS * ROWS

    own_master = masters[0]
    other_master = lax.ppermute(own_master, "grp", [(0, 1)])
    start = y * (2 * OWN_ROWS)
    lent_rows = lax.dynamic_slice_in_dim(features[0], start + (1 - grp) * OWN_ROWS, OWN_ROWS)
    other_rows = swapped(lent_rows)

    (pack,) = call(
        token_kernel,
        [shape((N_IMG, PACK, 256), jnp.bfloat16)],
        [],
        place,
        features[0],
        other_rows,
        patch_mask.reshape(4, 128),
    )
    packs = lax.all_to_all(pack, "img", 0, 0, tiled=True)

    master, unit = call(
        proto_kernel,
        [shape((BLOCK, 256)), shape((BLOCK, 256), jnp.bfloat16)],
        [],
        place,
        own_master,
        other_master,
    )
    own_units = [unit] + [from_y(unit, k) for k in range(1, N_Y)]
    other_units = [swapped(block) for block in own_units]

    teacher_exp, student_exp, col_parts, student_part, student_tokens, weights = call(
        exp_kernel,
        [
            shape((COLS, ROWS)),
            shape((COLS, ROWS)),
            shape((N_COLGRP, 16, 128)),
            shape((8, 128)),
            shape((ROWS, 256), jnp.bfloat16),
            shape((8, 128)),
        ],
        [
            pltpu.VMEM((ROWS, 256), jnp.bfloat16),
            pltpu.VMEM((16, 128), jnp.float32),
            pltpu.VMEM((8, ROWS), jnp.float32),
        ],
        place,
        packs,
        *own_units,
        *other_units,
        flops=4 * work * 256,
        transcendentals=2 * work,
    )

    for sweep in range(3):
        with_student = sweep == 0
        col_parts = exchange(col_parts, COL_GROUPS)
        row_parts, col_scale = call(
            functools.partial(row_kernel, with_student),
            [shape((N_ROWGRP, 16 if with_student else 8, 128)), shape((16, 128))],
            [],
            col_parts,
            teacher_exp,
            *((student_part,) if with_student else ()),
            flops=2 * work,
        )
        row_parts = exchange(row_parts, ROW_GROUPS)
        if sweep < 2:
            col_parts, *rest = call(
                functools.partial(col_kernel, with_student),
                [shape((N_COLGRP, 16, 128))] + [shape((8, 128))] * with_student,
                [pltpu.VMEM((16, 128), jnp.float32)],
                row_parts,
                teacher_exp,
                flops=2 * work,
            )
            if with_student:
                (student_inverse,) = rest

    own_grad, sent_grad = call(
        grad_kernel,
        [shape((COLS, 256)), shape((COLS, 256), jnp.bfloat16)],
        [],
        row_parts,
        col_scale,
        student_inverse,
        weights,
        teacher_exp,
        student_exp,
        student_tokens,
        flops=2 * work * 256,
    )
    received = lax.ppermute(sent_grad, "grp", [(1, 0)])
    mine, *outgoing = call(
        split_kernel,
        [shape((BLOCK, 256))] + [shape((BLOCK, 256), jnp.bfloat16)] * 3,
        [],
        place,
        own_grad,
        received,
    )
    gradient = mine
    for k, block in enumerate(outgoing, 1):
        gradient = gradient + from_y(block, -k, True).astype(jnp.float32)
    return jnp.where(teacher, master, gradient)[None]


def solution(mesh):
    in_specs = (P("grp", "img", None), P("grp", ("img", "tp"), None), P("img"))
    out_specs = P("grp", ("img", "tp"), None)
    return jax.shard_map(
        per_device, mesh=mesh, in_specs=in_specs, out_specs=out_specs, check_vma=False
    )
```

```python
import functools

import jax
import jax.numpy as jnp
from jax import lax
from jax.experimental import pallas as pl
from jax.experimental.pallas import tpu as pltpu
from jax.sharding import PartitionSpec as P

PROTOS = 65536
PATCHES = 256
MOMENTUM = 0.994
TEACHER_TEMP = 0.07
STUDENT_TEMP = 0.1
EPS = 1e-06
LOG2E = 1.4426950408889634

AXES = ("grp", "img", "tp")
N_GRP, N_IMG, N_TP = 2, 16, 8
N_X, N_Y, N_Z = 4, 4, 8
BLOCK = 512
HALF = 256
OWN_ROWS = 128
PACK = 2 * OWN_ROWS + 16
ROWS = N_Z * OWN_ROWS
COLS = N_X * BLOCK
N_ROWGRP = N_Y * N_Z
N_COLGRP = N_GRP * N_X
VMEM_LIMIT = 16 * 1024 * 1024


def coordinates(device):
    grp, rest = divmod(device, N_IMG * N_TP)
    img, tp = divmod(rest, N_TP)
    x_hi, z = divmod(img, N_Z)
    x_lo, y = divmod(tp, N_Y)
    return grp, x_hi * 2 + x_lo, y, z


def device_at(grp, x, y, z):
    return ((grp * 2 + x // 2) * N_Z + z) * N_TP + x % 2 * N_Y + y


def groups_of(key):
    found = {}
    for device in range(N_GRP * N_IMG * N_TP):
        found.setdefault(key(*coordinates(device)), []).append(device)
    return list(found.values())


X_GROUPS = groups_of(lambda grp, x, y, z: (grp, y, z))
COL_GROUPS = groups_of(lambda grp, x, y, z: (y, z))
ROW_GROUPS = groups_of(lambda grp, x, y, z: (grp, x))


def exchange(blocks, groups):
    return lax.all_to_all(blocks, AXES, 0, 0, axis_index_groups=groups, tiled=True)


def swapped(block):
    return lax.ppermute(block, "grp", [(0, 1), (1, 0)])


def from_x(block, distance):
    route = []
    for device in range(N_GRP * N_IMG * N_TP):
        grp, x, y, z = coordinates(device)
        route.append((device_at(grp, (x + distance) % N_X, y, z), device))
    return lax.ppermute(block, AXES, route)


def from_z(block, distance):
    route = []
    for device in range(N_GRP * N_IMG * N_TP):
        grp, x, y, z = coordinates(device)
        route.append((device_at(grp, x, y, (z + distance) % N_Z), device))
    return lax.ppermute(block, AXES, route)


def unit_rows(values):
    return (values / jnp.sqrt(jnp.sum(values * values, -1, keepdims=True) + EPS)).astype(
        jnp.bfloat16
    )


def diagonal():
    return lax.broadcasted_iota(jnp.int32, (128, 128), 0) == lax.broadcasted_iota(
        jnp.int32, (128, 128), 1
    )


def to_row(column):
    return jnp.sum(jnp.where(diagonal(), column, 0.0), axis=0, keepdims=True)


def to_column(row):
    return jnp.sum(jnp.where(diagonal(), row, 0.0), axis=1, keepdims=True)


def lanes(pieces):
    return jnp.concatenate([pieces[k : k + 1, :] for k in range(pieces.shape[0])], axis=1)


def pieces_of(row):
    return jnp.concatenate([row[:, k * 128 : (k + 1) * 128] for k in range(8)], axis=0)


def unit_kernel(
    place_ref,
    features_ref,
    other_features_ref,
    mask_ref,
    own_ref,
    other_ref,
    pack_ref,
    master_ref,
    unit_ref,
):
    grp, x = place_ref[0], place_ref[1]

    @pl.when(pl.program_id(0) == 0)
    def _():
        own = unit_rows(features_ref[...].astype(jnp.float32))
        other = unit_rows(other_features_ref[...].astype(jnp.float32))
        teacher = jnp.where(grp == 0, other, own)
        student = jnp.where(grp == 0, own, other)
        crop = mask_ref[pl.ds(x % 2 * 2, 2), :].astype(jnp.float32)
        count = jnp.maximum(jnp.sum(crop), 1.0)
        weight = mask_ref[pl.ds(x % 2 * 2 + grp, 1), :].astype(jnp.float32)
        weight = weight / (STUDENT_TEMP * count)
        weight = jnp.broadcast_to(jnp.concatenate([weight, weight], axis=1), (16, 256))
        weight = weight.astype(jnp.bfloat16)
        pack_ref[0:OWN_ROWS, :] = teacher
        pack_ref[OWN_ROWS : 2 * OWN_ROWS, :] = student
        pack_ref[2 * OWN_ROWS : PACK, :] = weight

    own_master = own_ref[...]
    blended = MOMENTUM * own_master + (1.0 - MOMENTUM) * other_ref[...]
    master = jnp.where(grp == 1, blended, own_master)
    master_ref[...] = master
    unit_ref[...] = unit_rows(master)


def in_hbm(array):
    return pltpu.with_memory_space_constraint(array, pltpu.HBM)


def unit_call(place, features, other_features, mask, own_master, other_master):
    rows = BLOCK // 4
    picked = pl.BlockSpec((OWN_ROWS, 256), lambda i, place: (place[1] % 2 * 2 + place[0], 0))
    part = pl.BlockSpec((rows, 256), lambda i, place: (i, 0))
    return pl.pallas_call(
        unit_kernel,
        out_shape=[
            shape((PACK, 256), jnp.bfloat16),
            shape((BLOCK, 256)),
            shape((BLOCK, 256), jnp.bfloat16),
        ],
        grid_spec=pltpu.PrefetchScalarGridSpec(
            num_scalar_prefetch=1,
            grid=(4,),
            in_specs=[
                picked,
                picked,
                pl.BlockSpec((4, 128), lambda i, place: (0, 0)),
                part,
                part,
            ],
            out_specs=[
                pl.BlockSpec((PACK, 256), lambda i, place: (0, 0)),
                part,
                part,
            ],
        ),
        compiler_params=pltpu.CompilerParams(vmem_limit_bytes=VMEM_LIMIT),
    )(place, in_hbm(features), other_features, mask, in_hbm(own_master), other_master)


def exp_of(protos, tokens, temperature):
    logits = lax.dot_general(
        protos, tokens, (((1,), (1,)), ((), ())), preferred_element_type=jnp.float32
    )
    return jnp.exp2(logits * (LOG2E / temperature))


def exp_kernel(*refs):
    place_ref, pack_refs = refs[0], refs[1:9]
    own_refs, other_refs = refs[9:13], refs[13:17]
    teacher_ref, student_ref, parts_ref, total_ref, token_ref, weight_ref = refs[17:23]
    scratch_ref, vector_ref = refs[23:]
    grp, x, z = place_ref[0], place_ref[1], place_ref[2]
    for k in range(N_Z):
        place = (z + k) % N_Z
        rows = pl.ds(pl.multiple_of(place * OWN_ROWS, OWN_ROWS), OWN_ROWS)
        scratch_ref[rows, :] = pack_refs[k][0:OWN_ROWS, :]
        token_ref[rows, :] = pack_refs[k][OWN_ROWS : 2 * OWN_ROWS, :]
        weight = pack_refs[k][2 * OWN_ROWS : PACK, 0:128].astype(jnp.float32)
        weight_ref[pl.ds(place, 1), :] = weight[0:1, :]
    teacher_tokens = scratch_ref[...]
    student_tokens = token_ref[...]
    total = jnp.zeros((8, ROWS), jnp.float32)
    for k in range(N_X):
        base = (x + k) % N_X * BLOCK
        for i in range(BLOCK // 256):
            block = slice(i * 256, (i + 1) * 256)
            rows = pl.ds(pl.multiple_of(base + i * 256, 256), 256)
            own, other = own_refs[k][block, :], other_refs[k][block, :]
            values = exp_of(jnp.where(grp == 0, other, own), teacher_tokens, TEACHER_TEMP)
            teacher_ref[rows, :] = values
            folded = sum(values[:, k * 128 : (k + 1) * 128] for k in range(8))
            column = jnp.sum(folded, axis=1, keepdims=True)
            for h in range(2):
                vector_ref[pl.ds(base // 128 + i * 2 + h, 1), :] = to_row(
                    column[h * 128 : (h + 1) * 128]
                )
            values = exp_of(jnp.where(grp == 0, own, other), student_tokens, STUDENT_TEMP)
            student_ref[rows, :] = values
            total += jnp.sum(values.reshape(32, 8, ROWS), axis=0)
    total_ref[...] = pieces_of(jnp.sum(total, axis=0, keepdims=True))
    for k in range(N_COLGRP):
        parts_ref[k] = vector_ref[...]


def row_kernel(with_student, *refs):
    if with_student:
        parts_ref, exp_ref, student_ref, out_ref, scale_ref = refs
    else:
        parts_ref, exp_ref, out_ref, scale_ref = refs
    scale = 1.0 / jnp.sum(parts_ref[...], axis=0)
    scale_ref[...] = scale
    total = jnp.zeros((8, ROWS), jnp.float32)
    for j in range(COLS // 128):
        weighted = exp_ref[j * 128 : (j + 1) * 128, :] * to_column(scale[j : j + 1, :])
        total += jnp.sum(weighted.reshape(16, 8, ROWS), axis=0)
    mine = pieces_of(jnp.sum(total, axis=0, keepdims=True))
    if with_student:
        mine = jnp.concatenate([mine, student_ref[...]], axis=0)
    mine = mine.astype(jnp.bfloat16)
    for k in range(N_ROWGRP):
        out_ref[k] = mine


def col_kernel(parts_ref, exp_ref, out_ref, vector_ref):
    row = lanes(1.0 / jnp.sum(parts_ref[...].astype(jnp.float32), axis=0))
    for j in range(COLS // 128):
        weighted = exp_ref[j * 128 : (j + 1) * 128, :] * row
        folded = sum(weighted[:, k * 128 : (k + 1) * 128] for k in range(8))
        vector_ref[j : j + 1, :] = to_row(jnp.sum(folded, axis=1, keepdims=True))
    for k in range(N_COLGRP):
        out_ref[k] = vector_ref[...]


def grad_kernel(
    other,
    place_ref,
    parts_ref,
    scale_ref,
    weight_ref,
    teacher_exp_ref,
    student_exp_ref,
    token_ref,
    out_ref,
):
    inverse = 1.0 / jnp.sum(parts_ref[...].astype(jnp.float32), axis=0)
    row_inverse, student_inverse = lanes(inverse[0:8, :]), lanes(inverse[8:16, :])
    weight = lanes(weight_ref[...])
    half = 1 - place_ref[0] if other else place_ref[0]
    for k in range(N_X):
        errors = []
        for h in range(2):
            start = k * BLOCK + half * HALF + h * 128
            column = to_column(scale_ref[pl.ds(start // 128, 1), :])
            rows = pl.ds(pl.multiple_of(start, 128), 128)
            targets = (teacher_exp_ref[rows, :] * column * row_inverse).astype(jnp.bfloat16)
            probs = student_exp_ref[rows, :] * student_inverse
            errors.append(
                (PROTOS * (probs - targets.astype(jnp.float32)) * weight).astype(jnp.bfloat16)
            )
        out_ref[k] = jnp.dot(
            jnp.concatenate(errors, axis=0), token_ref[...], preferred_element_type=jnp.float32
        ).astype(out_ref.dtype)


def call(kernel, outs, scratch, *args, flops=0, transcendentals=0):
    vmem = pl.BlockSpec(memory_space=pltpu.VMEM)
    smem = pl.BlockSpec(memory_space=pltpu.SMEM)
    return pl.pallas_call(
        kernel,
        out_shape=outs,
        in_specs=[smem if a.ndim == 1 else vmem for a in args],
        out_specs=[vmem] * len(outs),
        scratch_shapes=scratch,
        compiler_params=pltpu.CompilerParams(vmem_limit_bytes=VMEM_LIMIT),
        cost_estimate=pl.CostEstimate(
            flops=flops, transcendentals=transcendentals, bytes_accessed=COLS * ROWS * 4
        ),
    )(*args)


def shape(dims, dtype=jnp.float32):
    return jax.ShapeDtypeStruct(dims, dtype)


def per_device(features, masters, patch_mask):
    grp = lax.axis_index("grp")
    x = lax.axis_index("img") // N_Z * 2 + lax.axis_index("tp") // N_Y
    z = lax.axis_index("img") % N_Z
    place = jnp.stack([grp, x, z]).astype(jnp.int32)
    work = COLS * ROWS

    own_master = masters[0]
    other_master = lax.ppermute(own_master, "grp", [(0, 1)])
    other_features = swapped(features[0])
    pack, master, unit = unit_call(
        place,
        features[0],
        other_features,
        patch_mask.reshape(4, 128),
        own_master,
        other_master,
    )
    packs = {0: pack, 4: from_z(pack, 4), 1: from_z(pack, 1), 7: from_z(pack, -1)}
    packs[2], packs[5] = from_z(packs[1], 1), from_z(packs[4], 1)
    packs[6], packs[3] = from_z(packs[7], -1), from_z(packs[4], -1)
    own_units = [unit] + [from_x(unit, k) for k in range(1, N_X)]
    other_units = [swapped(block) for block in own_units]

    teacher_exp, student_exp, col_parts, student_part, student_tokens, weights = call(
        exp_kernel,
        [
            shape((COLS, ROWS)),
            shape((COLS, ROWS)),
            shape((N_COLGRP, 16, 128)),
            shape((8, 128)),
            shape((ROWS, 256), jnp.bfloat16),
            shape((8, 128)),
        ],
        [pltpu.VMEM((ROWS, 256), jnp.bfloat16), pltpu.VMEM((16, 128), jnp.float32)],
        place,
        *(packs[k] for k in range(N_Z)),
        *own_units,
        *other_units,
        flops=4 * work * 256,
        transcendentals=2 * work,
    )

    for sweep in range(3):
        last = sweep == 2
        col_parts = exchange(col_parts, COL_GROUPS)
        row_parts, col_scale = call(
            functools.partial(row_kernel, last),
            [shape((N_ROWGRP, 16 if last else 8, 128), jnp.bfloat16), shape((16, 128))],
            [],
            col_parts,
            teacher_exp,
            *((student_part,) if last else ()),
            flops=2 * work,
        )
        row_parts = exchange(row_parts, ROW_GROUPS)
        if not last:
            (col_parts,) = call(
                col_kernel,
                [shape((N_COLGRP, 16, 128))],
                [pltpu.VMEM((16, 128), jnp.float32)],
                row_parts,
                teacher_exp,
                flops=2 * work,
            )

    def partial_gradient(other, dtype):
        (out,) = call(
            functools.partial(grad_kernel, other),
            [shape((N_X, HALF, 256), dtype)],
            [],
            place,
            row_parts,
            col_scale,
            weights,
            teacher_exp,
            student_exp,
            student_tokens,
            flops=work * 256,
        )
        return out

    received = swapped(partial_gradient(True, jnp.bfloat16))
    chip = partial_gradient(False, jnp.float32) + received.astype(jnp.float32)
    pieces = exchange(chip.astype(jnp.bfloat16), X_GROUPS)
    half = jnp.sum(pieces.astype(jnp.float32), axis=0)
    second = lax.ppermute(half, "grp", [(1, 0)])
    return jnp.where(grp == 1, master, jnp.concatenate([half, second]))[None]


def solution(mesh):
    in_specs = (P("grp", "img", None), P("grp", ("img", "tp"), None), P("img"))
    out_specs = P("grp", ("img", "tp"), None)
    return jax.shard_map(
        per_device, mesh=mesh, in_specs=in_specs, out_specs=out_specs, check_vma=False
    )
```

```python
import functools

import jax
import jax.numpy as jnp
from jax import lax
from jax.experimental import pallas as pl
from jax.experimental.pallas import tpu as pltpu
from jax.sharding import PartitionSpec as P

PROTOS = 65536
PATCHES = 256
MOMENTUM = 0.994
TEACHER_TEMP = 0.07
STUDENT_TEMP = 0.1
EPS = 1e-06
LOG2E = 1.4426950408889634

AXES = ("grp", "img", "tp")
N_GRP, N_IMG, N_TP = 2, 16, 8
N_X, N_Y, N_Z = 4, 4, 8
BLOCK = 512
HALF = 256
OWN_ROWS = 128
PACK = 2 * OWN_ROWS
ROWS = N_Z * OWN_ROWS
COLS = N_X * BLOCK
N_ROWGRP = N_Y * N_Z
N_COLGRP = N_GRP * N_X
VMEM_LIMIT = 16 * 1024 * 1024


def coordinates(device):
    grp, rest = divmod(device, N_IMG * N_TP)
    img, tp = divmod(rest, N_TP)
    x_hi, z = divmod(img, N_Z)
    x_lo, y = divmod(tp, N_Y)
    return grp, x_hi * 2 + x_lo, y, z


def device_at(grp, x, y, z):
    return ((grp * 2 + x // 2) * N_Z + z) * N_TP + x % 2 * N_Y + y


def groups_of(key):
    found = {}
    for device in range(N_GRP * N_IMG * N_TP):
        found.setdefault(key(*coordinates(device)), []).append(device)
    return list(found.values())


COL_GROUPS = groups_of(lambda grp, x, y, z: (y, z))
ROW_GROUPS = groups_of(lambda grp, x, y, z: (grp, x))


def exchange(blocks, groups):
    return lax.all_to_all(blocks, AXES, 0, 0, axis_index_groups=groups, tiled=True)


def swapped(block):
    return lax.ppermute(block, "grp", [(0, 1), (1, 0)])


def permuted(block, target_of):
    route = []
    for device in range(N_GRP * N_IMG * N_TP):
        target = target_of(*coordinates(device))
        if target is not None:
            route.append((device, device_at(*target)))
    return lax.ppermute(block, AXES, route)


def from_x(block, distance):
    return permuted(block, lambda grp, x, y, z: (grp, (x - distance) % N_X, y, z))


def from_z(block, distance):
    return permuted(block, lambda grp, x, y, z: (grp, x, y, (z - distance) % N_Z))


def unit_rows(values):
    return (values / jnp.sqrt(jnp.sum(values * values, -1, keepdims=True) + EPS)).astype(
        jnp.bfloat16
    )


def diagonal():
    return lax.broadcasted_iota(jnp.int32, (128, 128), 0) == lax.broadcasted_iota(
        jnp.int32, (128, 128), 1
    )


def to_row(column):
    return jnp.sum(jnp.where(diagonal(), column, 0.0), axis=0, keepdims=True)


def to_column(row):
    return jnp.sum(jnp.where(diagonal(), row, 0.0), axis=1, keepdims=True)


def lanes(pieces):
    return jnp.concatenate([pieces[k : k + 1, :] for k in range(pieces.shape[0])], axis=1)


def pieces_of(row):
    return jnp.concatenate([row[:, k * 128 : (k + 1) * 128] for k in range(8)], axis=0)


def unit_kernel(
    place_ref,
    features_ref,
    other_features_ref,
    mask_ref,
    own_ref,
    other_ref,
    pack_ref,
    weight_ref,
    unit_ref,
):
    grp, x = place_ref[0], place_ref[1]

    @pl.when(pl.program_id(0) == 0)
    def _():
        own = unit_rows(features_ref[...].astype(jnp.float32))
        other = unit_rows(other_features_ref[...].astype(jnp.float32))
        teacher = jnp.where(grp == 0, other, own)
        student = jnp.where(grp == 0, own, other)
        crop = mask_ref[pl.ds(x % 2 * 2, 2), :].astype(jnp.float32)
        count = jnp.maximum(jnp.sum(crop), 1.0)
        weight = mask_ref[pl.ds(x % 2 * 2 + grp, 1), :].astype(jnp.float32)
        weight = weight / (STUDENT_TEMP * count)
        weight_ref[...] = jnp.broadcast_to(weight, (8, 128)).astype(jnp.bfloat16)
        pack_ref[0:OWN_ROWS, :] = teacher
        pack_ref[OWN_ROWS:PACK, :] = student

    own_master = own_ref[...]
    blended = MOMENTUM * own_master + (1.0 - MOMENTUM) * other_ref[...]
    master = jnp.where(grp == 1, blended, own_master)
    unit_ref[...] = unit_rows(master)


def in_hbm(array):
    return pltpu.with_memory_space_constraint(array, pltpu.HBM)


def unit_call(place, features, other_features, mask, own_master, other_master):
    rows = BLOCK // 2
    picked = pl.BlockSpec((OWN_ROWS, 256), lambda i, place: (place[1] % 2 * 2 + place[0], 0))
    part = pl.BlockSpec((rows, 256), lambda i, place: (i, 0))
    return pl.pallas_call(
        unit_kernel,
        out_shape=[
            shape((PACK, 256), jnp.bfloat16),
            shape((8, 128), jnp.bfloat16),
            shape((BLOCK, 256), jnp.bfloat16),
        ],
        grid_spec=pltpu.PrefetchScalarGridSpec(
            num_scalar_prefetch=1,
            grid=(2,),
            in_specs=[
                picked,
                picked,
                pl.BlockSpec((4, 128), lambda i, place: (0, 0)),
                part,
                part,
            ],
            out_specs=[
                pl.BlockSpec((PACK, 256), lambda i, place: (0, 0)),
                pl.BlockSpec((8, 128), lambda i, place: (0, 0)),
                part,
            ],
        ),
        compiler_params=pltpu.CompilerParams(vmem_limit_bytes=VMEM_LIMIT),
    )(place, in_hbm(features), other_features, in_hbm(mask), in_hbm(own_master), other_master)


def exp_of(protos, tokens, temperature):
    logits = lax.dot_general(
        protos, tokens, (((1,), (1,)), ((), ())), preferred_element_type=jnp.float32
    )
    return jnp.exp2(logits * (LOG2E / temperature))


def exp_kernel(*refs):
    place_ref, pack_refs = refs[0], refs[1:9]
    own_refs, other_refs = refs[9:13], refs[13:17]
    teacher_ref, student_ref, parts_ref, total_ref, token_ref = refs[17:22]
    scratch_ref, vector_ref = refs[22:]
    grp, x, z = place_ref[0], place_ref[1], place_ref[2]
    for k in range(N_Z):
        rows = pl.ds(pl.multiple_of((z + k) % N_Z * OWN_ROWS, OWN_ROWS), OWN_ROWS)
        scratch_ref[rows, :] = pack_refs[k][0:OWN_ROWS, :]
        token_ref[rows, :] = pack_refs[k][OWN_ROWS:PACK, :]
    teacher_tokens = scratch_ref[...]
    student_tokens = token_ref[...]
    total = jnp.zeros((8, ROWS), jnp.float32)
    for k in range(N_X):
        base = (x + k) % N_X * BLOCK
        for i in range(BLOCK // 256):
            block = slice(i * 256, (i + 1) * 256)
            rows = pl.ds(pl.multiple_of(base + i * 256, 256), 256)
            own, other = own_refs[k][block, :], other_refs[k][block, :]
            values = exp_of(jnp.where(grp == 0, other, own), teacher_tokens, TEACHER_TEMP)
            teacher_ref[rows, :] = values
            folded = sum(values[:, k * 128 : (k + 1) * 128] for k in range(8))
            column = jnp.sum(folded, axis=1, keepdims=True)
            for h in range(2):
                vector_ref[pl.ds(base // 128 + i * 2 + h, 1), :] = to_row(
                    column[h * 128 : (h + 1) * 128]
                )
            values = exp_of(jnp.where(grp == 0, own, other), student_tokens, STUDENT_TEMP)
            student_ref[rows, :] = values
            total += jnp.sum(values.reshape(32, 8, ROWS), axis=0)
    total_ref[...] = pieces_of(jnp.sum(total, axis=0, keepdims=True))
    for k in range(N_COLGRP):
        parts_ref[k] = vector_ref[...]


def row_kernel(with_extra, *refs):
    if with_extra:
        parts_ref, exp_ref, extra_ref, out_ref, scale_ref = refs
    else:
        parts_ref, exp_ref, out_ref, scale_ref = refs
    scale = 1.0 / jnp.sum(parts_ref[...], axis=0)
    scale_ref[...] = scale
    total = jnp.zeros((8, ROWS), jnp.float32)
    for j in range(COLS // 128):
        weighted = exp_ref[j * 128 : (j + 1) * 128, :] * to_column(scale[j : j + 1, :])
        total += jnp.sum(weighted.reshape(16, 8, ROWS), axis=0)
    mine = pieces_of(jnp.sum(total, axis=0, keepdims=True))
    if with_extra:
        mine = jnp.concatenate([mine, extra_ref[...].astype(jnp.float32)], axis=0)
    mine = mine.astype(jnp.bfloat16)
    for k in range(N_ROWGRP):
        out_ref[k] = mine


def col_kernel(with_weight, *refs):
    if with_weight:
        parts_ref, exp_ref, out_ref, weight_ref, vector_ref = refs
        for z in range(N_Z):
            extra = parts_ref[z * N_Y, 8:16, :].astype(jnp.float32)
            weight_ref[z : z + 1, :] = extra[0:1, :]
    else:
        parts_ref, exp_ref, out_ref, vector_ref = refs
    row = lanes(1.0 / jnp.sum(parts_ref[:, 0:8, :].astype(jnp.float32), axis=0))
    for j in range(COLS // 128):
        weighted = exp_ref[j * 128 : (j + 1) * 128, :] * row
        folded = sum(weighted[:, k * 128 : (k + 1) * 128] for k in range(8))
        vector_ref[j : j + 1, :] = to_row(jnp.sum(folded, axis=1, keepdims=True))
    for k in range(N_COLGRP):
        out_ref[k] = vector_ref[...]


def grad_kernel(
    other,
    place_ref,
    parts_ref,
    scale_ref,
    weight_ref,
    teacher_exp_ref,
    student_exp_ref,
    token_ref,
    out_ref,
):
    inverse = 1.0 / jnp.sum(parts_ref[...].astype(jnp.float32), axis=0)
    row_inverse, student_inverse = lanes(inverse[0:8, :]), lanes(inverse[8:16, :])
    weight = lanes(weight_ref[...])
    first = 1 - place_ref[0] if other else place_ref[0]
    for k in range(2):
        base = (place_ref[1] + 2 * k + first) % N_X * BLOCK
        for i in range(BLOCK // 256):
            errors = []
            for h in range(2):
                start = base + i * 256 + h * 128
                column = to_column(scale_ref[pl.ds(start // 128, 1), :])
                rows = pl.ds(pl.multiple_of(start, 128), 128)
                targets = (teacher_exp_ref[rows, :] * column * row_inverse).astype(jnp.bfloat16)
                probs = student_exp_ref[rows, :] * student_inverse
                errors.append(
                    (PROTOS * (probs - targets.astype(jnp.float32)) * weight).astype(jnp.bfloat16)
                )
            out_ref[k, i * 256 : (i + 1) * 256, :] = jnp.dot(
                jnp.concatenate(errors, axis=0),
                token_ref[...],
                preferred_element_type=jnp.float32,
            ).astype(out_ref.dtype)


def call(kernel, outs, scratch, *args, flops=0, transcendentals=0):
    vmem = pl.BlockSpec(memory_space=pltpu.VMEM)
    smem = pl.BlockSpec(memory_space=pltpu.SMEM)
    return pl.pallas_call(
        kernel,
        out_shape=outs,
        in_specs=[smem if a.ndim == 1 else vmem for a in args],
        out_specs=[vmem] * len(outs),
        scratch_shapes=scratch,
        compiler_params=pltpu.CompilerParams(vmem_limit_bytes=VMEM_LIMIT),
        cost_estimate=pl.CostEstimate(
            flops=flops, transcendentals=transcendentals, bytes_accessed=COLS * ROWS * 4
        ),
    )(*args)


def shape(dims, dtype=jnp.float32):
    return jax.ShapeDtypeStruct(dims, dtype)


def per_device(features, masters, patch_mask):
    grp = lax.axis_index("grp")
    x = lax.axis_index("img") // N_Z * 2 + lax.axis_index("tp") // N_Y
    z = lax.axis_index("img") % N_Z
    place = jnp.stack([grp, x, z]).astype(jnp.int32)
    work = COLS * ROWS

    own_master = masters[0]
    other_master = lax.ppermute(own_master, "grp", [(0, 1)])
    other_features = swapped(features[0])
    pack, weight, unit = unit_call(
        place,
        features[0],
        other_features,
        patch_mask.reshape(4, 128),
        own_master,
        other_master,
    )
    packs = {0: pack, 4: from_z(pack, 4), 1: from_z(pack, 1), 7: from_z(pack, -1)}
    packs[2], packs[5] = from_z(packs[1], 1), from_z(packs[4], 1)
    packs[6], packs[3] = from_z(packs[7], -1), from_z(packs[4], -1)
    own_units = [unit] + [from_x(unit, k) for k in range(1, N_X)]
    held, packs = lax.optimization_barrier((tuple(own_units), packs))
    other_units = [swapped(block) for block in held]

    teacher_exp, student_exp, col_parts, student_part, student_tokens = call(
        exp_kernel,
        [
            shape((COLS, ROWS)),
            shape((COLS, ROWS)),
            shape((N_COLGRP, 16, 128)),
            shape((8, 128)),
            shape((ROWS, 256), jnp.bfloat16),
        ],
        [pltpu.VMEM((ROWS, 256), jnp.bfloat16), pltpu.VMEM((16, 128), jnp.float32)],
        place,
        *(packs[k] for k in range(N_Z)),
        *own_units,
        *other_units,
        flops=4 * work * 256,
        transcendentals=2 * work,
    )

    for sweep in range(3):
        first, last = sweep == 0, sweep == 2
        extra = (weight,) if first else (student_part,) if last else ()
        col_parts = exchange(col_parts, COL_GROUPS)
        row_parts, col_scale = call(
            functools.partial(row_kernel, first or last),
            [shape((N_ROWGRP, 16 if extra else 8, 128), jnp.bfloat16), shape((16, 128))],
            [],
            col_parts,
            teacher_exp,
            *extra,
            flops=2 * work,
        )
        row_parts = exchange(row_parts, ROW_GROUPS)
        if not last:
            col_parts, *rest = call(
                functools.partial(col_kernel, first),
                [shape((N_COLGRP, 16, 128))] + [shape((8, 128))] * first,
                [pltpu.VMEM((16, 128), jnp.float32)],
                row_parts,
                teacher_exp,
                flops=2 * work,
            )
            if first:
                (weights,) = rest

    def partial_gradient(other, dtype):
        (out,) = call(
            functools.partial(grad_kernel, other),
            [shape((2, BLOCK, 256), dtype)],
            [],
            place,
            row_parts,
            col_scale,
            weights,
            teacher_exp,
            student_exp,
            student_tokens,
            flops=work * 256,
        )
        return out

    received = swapped(partial_gradient(True, jnp.bfloat16))
    chip = partial_gradient(False, jnp.float32) + received.astype(jnp.float32)
    near, far = chip[0].astype(jnp.bfloat16), chip[1].astype(jnp.bfloat16)

    def sent(block, source, distance):
        return permuted(
            block,
            lambda grp, x, y, z: (0, (x + distance) % N_X, y, z) if grp == source else None,
        ).astype(jnp.float32)

    gradient = chip[0] + sent(far, 0, 2) + sent(near, 1, 1) + sent(far, 1, 3)
    blended = MOMENTUM * own_master + (1.0 - MOMENTUM) * other_master
    return jnp.where(grp == 1, blended, gradient)[None]


def solution(mesh):
    in_specs = (P("grp", "img", None), P("grp", ("img", "tp"), None), P("img"))
    out_specs = P("grp", ("img", "tp"), None)
    return jax.shard_map(
        per_device, mesh=mesh, in_specs=in_specs, out_specs=out_specs, check_vma=False
    )
```

```python
import functools

import jax
import jax.numpy as jnp
from jax import lax
from jax.experimental import pallas as pl
from jax.experimental.pallas import tpu as pltpu
from jax.sharding import PartitionSpec as P

PROTOS = 65536
PATCHES = 256
MOMENTUM = 0.994
TEACHER_TEMP = 0.07
STUDENT_TEMP = 0.1
EPS = 1e-06
LOG2E = 1.4426950408889634

AXES = ("grp", "img", "tp")
N_GRP, N_IMG, N_TP = 2, 16, 8
N_X, N_Y, N_Z = 4, 4, 8
BLOCK = 512
HALF = 256
OWN_ROWS = 128
PACK = 2 * OWN_ROWS
ROWS = N_Z * OWN_ROWS
COLS = N_X * BLOCK
N_ROWGRP = N_Y * N_Z
N_COLGRP = N_GRP * N_X
VMEM_LIMIT = 16 * 1024 * 1024


def coordinates(device):
    grp, rest = divmod(device, N_IMG * N_TP)
    img, tp = divmod(rest, N_TP)
    x_hi, z = divmod(img, N_Z)
    x_lo, y = divmod(tp, N_Y)
    return grp, x_hi * 2 + x_lo, y, z


def device_at(grp, x, y, z):
    return ((grp * 2 + x // 2) * N_Z + z) * N_TP + x % 2 * N_Y + y


def groups_of(key):
    found = {}
    for device in range(N_GRP * N_IMG * N_TP):
        found.setdefault(key(*coordinates(device)), []).append(device)
    return list(found.values())


COL_GROUPS = groups_of(lambda grp, x, y, z: (y, z))
ROW_GROUPS = groups_of(lambda grp, x, y, z: (grp, x))


def exchange(blocks, groups):
    return lax.all_to_all(blocks, AXES, 0, 0, axis_index_groups=groups, tiled=True)


def swapped(block):
    return lax.ppermute(block, "grp", [(0, 1), (1, 0)])


def permuted(block, target_of):
    route = []
    for device in range(N_GRP * N_IMG * N_TP):
        target = target_of(*coordinates(device))
        if target is not None:
            route.append((device, device_at(*target)))
    return lax.ppermute(block, AXES, route)


def from_x(block, distance):
    return permuted(block, lambda grp, x, y, z: (grp, (x - distance) % N_X, y, z))


def from_z(block, distance):
    return permuted(block, lambda grp, x, y, z: (grp, x, y, (z - distance) % N_Z))


def unit_rows(values):
    return (values / jnp.sqrt(jnp.sum(values * values, -1, keepdims=True) + EPS)).astype(
        jnp.bfloat16
    )


def diagonal():
    return lax.broadcasted_iota(jnp.int32, (128, 128), 0) == lax.broadcasted_iota(
        jnp.int32, (128, 128), 1
    )


def to_row(column):
    return jnp.sum(jnp.where(diagonal(), column, 0.0), axis=0, keepdims=True)


def to_column(row):
    return jnp.sum(jnp.where(diagonal(), row, 0.0), axis=1, keepdims=True)


def lanes(pieces):
    return jnp.concatenate([pieces[k : k + 1, :] for k in range(pieces.shape[0])], axis=1)


def pieces_of(row):
    return jnp.concatenate([row[:, k * 128 : (k + 1) * 128] for k in range(8)], axis=0)


def unit_kernel(
    place_ref,
    features_ref,
    other_features_ref,
    mask_ref,
    own_ref,
    other_ref,
    pack_ref,
    weight_ref,
    unit_ref,
):
    grp, x = place_ref[0], place_ref[1]

    @pl.when(pl.program_id(0) == 0)
    def _():
        own = unit_rows(features_ref[...].astype(jnp.float32))
        other = unit_rows(other_features_ref[...].astype(jnp.float32))
        teacher = jnp.where(grp == 0, other, own)
        student = jnp.where(grp == 0, own, other)
        crop = mask_ref[pl.ds(x % 2 * 2, 2), :].astype(jnp.float32)
        count = jnp.maximum(jnp.sum(crop), 1.0)
        weight = mask_ref[pl.ds(x % 2 * 2 + grp, 1), :].astype(jnp.float32)
        weight = weight / (STUDENT_TEMP * count)
        weight_ref[...] = jnp.broadcast_to(weight, (8, 128)).astype(jnp.bfloat16)
        pack_ref[0:OWN_ROWS, :] = teacher
        pack_ref[OWN_ROWS:PACK, :] = student

    own_master = own_ref[...]
    blended = MOMENTUM * own_master + (1.0 - MOMENTUM) * other_ref[...]
    master = jnp.where(grp == 1, blended, own_master)
    unit_ref[...] = unit_rows(master)


def in_hbm(array):
    return pltpu.with_memory_space_constraint(array, pltpu.HBM)


def unit_call(place, features, other_features, mask, own_master, other_master):
    rows = BLOCK // 2
    picked = pl.BlockSpec((OWN_ROWS, 256), lambda i, place: (place[1] % 2 * 2 + place[0], 0))
    part = pl.BlockSpec((rows, 256), lambda i, place: (i, 0))
    return pl.pallas_call(
        unit_kernel,
        out_shape=[
            shape((PACK, 256), jnp.bfloat16),
            shape((8, 128), jnp.bfloat16),
            shape((BLOCK, 256), jnp.bfloat16),
        ],
        grid_spec=pltpu.PrefetchScalarGridSpec(
            num_scalar_prefetch=1,
            grid=(2,),
            in_specs=[
                picked,
                picked,
                pl.BlockSpec((4, 128), lambda i, place: (0, 0)),
                part,
                part,
            ],
            out_specs=[
                pl.BlockSpec((PACK, 256), lambda i, place: (0, 0)),
                pl.BlockSpec((8, 128), lambda i, place: (0, 0)),
                part,
            ],
        ),
        compiler_params=pltpu.CompilerParams(vmem_limit_bytes=VMEM_LIMIT),
    )(place, in_hbm(features), other_features, in_hbm(mask), in_hbm(own_master), other_master)


def exp_of(protos, tokens, temperature):
    logits = lax.dot_general(
        protos, tokens, (((1,), (1,)), ((), ())), preferred_element_type=jnp.float32
    )
    return jnp.exp2(logits * (LOG2E / temperature))


def exp_kernel(*refs):
    place_ref, pack_refs = refs[0], refs[1:9]
    own_refs, other_refs = refs[9:13], refs[13:17]
    teacher_ref, student_ref, parts_ref, total_ref, token_ref = refs[17:22]
    scratch_ref, vector_ref = refs[22:]
    grp, x, z = place_ref[0], place_ref[1], place_ref[2]
    for k in range(N_Z):
        rows = pl.ds(pl.multiple_of((z + k) % N_Z * OWN_ROWS, OWN_ROWS), OWN_ROWS)
        scratch_ref[rows, :] = pack_refs[k][0:OWN_ROWS, :]
        token_ref[rows, :] = pack_refs[k][OWN_ROWS:PACK, :]
    teacher_tokens = scratch_ref[...]
    student_tokens = token_ref[...]
    total = jnp.zeros((8, ROWS), jnp.float32)
    for k in range(N_X):
        base = (x + k) % N_X * BLOCK
        for i in range(BLOCK // 256):
            block = slice(i * 256, (i + 1) * 256)
            rows = pl.ds(pl.multiple_of(base + i * 256, 256), 256)
            own, other = own_refs[k][block, :], other_refs[k][block, :]
            values = exp_of(jnp.where(grp == 0, other, own), teacher_tokens, TEACHER_TEMP)
            teacher_ref[rows, :] = values
            folded = sum(values[:, k * 128 : (k + 1) * 128] for k in range(8))
            column = jnp.sum(folded, axis=1, keepdims=True)
            for h in range(2):
                vector_ref[pl.ds(base // 128 + i * 2 + h, 1), :] = to_row(
                    column[h * 128 : (h + 1) * 128]
                )
            values = exp_of(jnp.where(grp == 0, own, other), student_tokens, STUDENT_TEMP)
            student_ref[rows, :] = values
            total += jnp.sum(values.reshape(32, 8, ROWS), axis=0)
    total_ref[...] = pieces_of(jnp.sum(total, axis=0, keepdims=True))
    for k in range(N_COLGRP):
        parts_ref[k] = vector_ref[...]


def row_kernel(with_extra, *refs):
    if with_extra:
        parts_ref, exp_ref, extra_ref, out_ref, scale_ref = refs
    else:
        parts_ref, exp_ref, out_ref, scale_ref = refs
    scale = 1.0 / jnp.sum(parts_ref[...], axis=0)
    scale_ref[...] = scale
    total = jnp.zeros((8, ROWS), jnp.float32)
    for j in range(COLS // 128):
        weighted = exp_ref[j * 128 : (j + 1) * 128, :] * to_column(scale[j : j + 1, :])
        total += jnp.sum(weighted.reshape(16, 8, ROWS), axis=0)
    mine = pieces_of(jnp.sum(total, axis=0, keepdims=True))
    if with_extra:
        mine = jnp.concatenate([mine, extra_ref[...].astype(jnp.float32)], axis=0)
    mine = mine.astype(jnp.bfloat16)
    for k in range(N_ROWGRP):
        out_ref[k] = mine


def col_kernel(with_weight, *refs):
    if with_weight:
        parts_ref, exp_ref, out_ref, weight_ref, vector_ref = refs
        for z in range(N_Z):
            extra = parts_ref[z * N_Y, 8:16, :].astype(jnp.float32)
            weight_ref[z : z + 1, :] = extra[0:1, :]
    else:
        parts_ref, exp_ref, out_ref, vector_ref = refs
    row = lanes(1.0 / jnp.sum(parts_ref[:, 0:8, :].astype(jnp.float32), axis=0))
    for j in range(COLS // 128):
        weighted = exp_ref[j * 128 : (j + 1) * 128, :] * row
        folded = sum(weighted[:, k * 128 : (k + 1) * 128] for k in range(8))
        vector_ref[j : j + 1, :] = to_row(jnp.sum(folded, axis=1, keepdims=True))
    for k in range(N_COLGRP):
        out_ref[k] = vector_ref[...]


def grad_kernel(
    other,
    pieces,
    place_ref,
    parts_ref,
    scale_ref,
    weight_ref,
    teacher_exp_ref,
    student_exp_ref,
    token_ref,
    out_ref,
):
    inverse = 1.0 / jnp.sum(parts_ref[...].astype(jnp.float32), axis=0)
    row_inverse, student_inverse = lanes(inverse[0:8, :]), lanes(inverse[8:16, :])
    weight = lanes(weight_ref[...] * PROTOS)
    teacher_row, student_row = row_inverse * weight, student_inverse * weight
    first = 1 - place_ref[0] if other else place_ref[0]
    for n, k in enumerate(pieces):
        base = (place_ref[1] + 2 * k + first) % N_X * BLOCK
        for i in range(BLOCK // 256):
            errors = []
            for h in range(2):
                start = base + i * 256 + h * 128
                column = to_column(scale_ref[pl.ds(start // 128, 1), :])
                rows = pl.ds(pl.multiple_of(start, 128), 128)
                targets = teacher_exp_ref[rows, :] * column * teacher_row
                probs = student_exp_ref[rows, :] * student_row
                errors.append((probs - targets).astype(jnp.bfloat16))
            out_ref[n, i * 256 : (i + 1) * 256, :] = jnp.dot(
                jnp.concatenate(errors, axis=0),
                token_ref[...],
                preferred_element_type=jnp.float32,
            ).astype(out_ref.dtype)


def call(kernel, outs, scratch, *args, flops=0, transcendentals=0):
    vmem = pl.BlockSpec(memory_space=pltpu.VMEM)
    smem = pl.BlockSpec(memory_space=pltpu.SMEM)
    return pl.pallas_call(
        kernel,
        out_shape=outs,
        in_specs=[smem if a.ndim == 1 else vmem for a in args],
        out_specs=[vmem] * len(outs),
        scratch_shapes=scratch,
        compiler_params=pltpu.CompilerParams(vmem_limit_bytes=VMEM_LIMIT),
        cost_estimate=pl.CostEstimate(
            flops=flops, transcendentals=transcendentals, bytes_accessed=COLS * ROWS * 4
        ),
    )(*args)


def shape(dims, dtype=jnp.float32):
    return jax.ShapeDtypeStruct(dims, dtype)


def per_device(features, masters, patch_mask):
    grp = lax.axis_index("grp")
    x = lax.axis_index("img") // N_Z * 2 + lax.axis_index("tp") // N_Y
    z = lax.axis_index("img") % N_Z
    place = jnp.stack([grp, x, z]).astype(jnp.int32)
    work = COLS * ROWS

    own_master = masters[0]
    other_master = lax.ppermute(own_master, "grp", [(0, 1)])
    other_features = swapped(features[0])
    pack, weight, unit = unit_call(
        place,
        features[0],
        other_features,
        patch_mask.reshape(4, 128),
        own_master,
        other_master,
    )
    packs = {0: pack}
    for k in range(1, 5):
        packs[k] = from_z(packs[k - 1], 1)
        if k < 4:
            packs[N_Z - k] = from_z(packs[(N_Z - k + 1) % N_Z], -1)
    own_units = [unit, from_x(unit, 1), None, from_x(unit, -1)]
    own_units[2] = from_x(own_units[1], 1)
    held, packs = lax.optimization_barrier((tuple(own_units[1:]), packs))
    other_units = [swapped(unit)] + [swapped(block) for block in held]

    teacher_exp, student_exp, col_parts, student_part, student_tokens = call(
        exp_kernel,
        [
            shape((COLS, ROWS)),
            shape((COLS, ROWS)),
            shape((N_COLGRP, 16, 128)),
            shape((8, 128)),
            shape((ROWS, 256), jnp.bfloat16),
        ],
        [pltpu.VMEM((ROWS, 256), jnp.bfloat16), pltpu.VMEM((16, 128), jnp.float32)],
        place,
        *(packs[k] for k in range(N_Z)),
        *own_units,
        *other_units,
        flops=4 * work * 256,
        transcendentals=2 * work,
    )

    for sweep in range(3):
        first, last = sweep == 0, sweep == 2
        extra = (weight,) if first else (student_part,) if last else ()
        col_parts = exchange(col_parts, COL_GROUPS)
        row_parts, col_scale = call(
            functools.partial(row_kernel, first or last),
            [shape((N_ROWGRP, 16 if extra else 8, 128), jnp.bfloat16), shape((16, 128))],
            [],
            col_parts,
            teacher_exp,
            *extra,
            flops=2 * work,
        )
        row_parts = exchange(row_parts, ROW_GROUPS)
        if not last:
            col_parts, *rest = call(
                functools.partial(col_kernel, first),
                [shape((N_COLGRP, 16, 128))] + [shape((8, 128))] * first,
                [pltpu.VMEM((16, 128), jnp.float32)],
                row_parts,
                teacher_exp,
                flops=2 * work,
            )
            if first:
                (weights,) = rest

    def partial_gradient(other, pieces, dtype):
        (out,) = call(
            functools.partial(grad_kernel, other, pieces),
            [shape((len(pieces), BLOCK, 256), dtype)],
            [],
            place,
            row_parts,
            col_scale,
            weights,
            teacher_exp,
            student_exp,
            student_tokens,
            flops=work * 256,
        )
        return out

    received = swapped(partial_gradient(True, (0, 1), jnp.bfloat16))
    chip = partial_gradient(False, (0, 1), jnp.float32) + received.astype(jnp.float32)
    near, far = chip[0].astype(jnp.bfloat16), chip[1].astype(jnp.bfloat16)

    def sent(block, source, distance):
        return permuted(
            block,
            lambda grp, x, y, z: (0, (x + distance) % N_X, y, z) if grp == source else None,
        ).astype(jnp.float32)

    gradient = chip[0] + sent(far, 0, 2) + sent(near, 1, 1) + sent(far, 1, 3)
    blended = MOMENTUM * own_master + (1.0 - MOMENTUM) * other_master
    return jnp.where(grp == 1, blended, gradient)[None]


def solution(mesh):
    in_specs = (P("grp", "img", None), P("grp", ("img", "tp"), None), P("img"))
    out_specs = P("grp", ("img", "tp"), None)
    return jax.shard_map(
        per_device, mesh=mesh, in_specs=in_specs, out_specs=out_specs, check_vma=False
    )
```

```python
import functools

import jax
import jax.numpy as jnp
from jax import lax
from jax.experimental import pallas as pl
from jax.experimental.pallas import tpu as pltpu
from jax.sharding import PartitionSpec as P

PROTOS = 65536
PATCHES = 256
MOMENTUM = 0.994
TEACHER_TEMP = 0.07
STUDENT_TEMP = 0.1
EPS = 1e-06
LOG2E = 1.4426950408889634

AXES = ("grp", "img", "tp")
N_GRP, N_IMG, N_TP = 2, 16, 8
N_X, N_Y, N_Z = 4, 4, 8
BLOCK = 512
HALF = 256
OWN_ROWS = 128
PACK = 2 * OWN_ROWS
ROWS = N_Z * OWN_ROWS
COLS = N_X * BLOCK
N_ROWGRP = N_Y * N_Z
N_COLGRP = N_GRP * N_X
VMEM_LIMIT = 16 * 1024 * 1024


def coordinates(device):
    grp, rest = divmod(device, N_IMG * N_TP)
    img, tp = divmod(rest, N_TP)
    x_hi, z = divmod(img, N_Z)
    x_lo, y = divmod(tp, N_Y)
    return grp, x_hi * 2 + x_lo, y, z


def device_at(grp, x, y, z):
    return ((grp * 2 + x // 2) * N_Z + z) * N_TP + x % 2 * N_Y + y


def groups_of(key):
    found = {}
    for device in range(N_GRP * N_IMG * N_TP):
        found.setdefault(key(*coordinates(device)), []).append(device)
    return list(found.values())


COL_GROUPS = groups_of(lambda grp, x, y, z: (y, z))
ROW_GROUPS = groups_of(lambda grp, x, y, z: (grp, x))


def exchange(blocks, groups):
    return lax.all_to_all(blocks, AXES, 0, 0, axis_index_groups=groups, tiled=True)


def swapped(block):
    return lax.ppermute(block, "grp", [(0, 1), (1, 0)])


def permuted(block, target_of):
    route = []
    for device in range(N_GRP * N_IMG * N_TP):
        target = target_of(*coordinates(device))
        if target is not None:
            route.append((device, device_at(*target)))
    return lax.ppermute(block, AXES, route)


def from_x(block, distance):
    return permuted(block, lambda grp, x, y, z: (grp, (x - distance) % N_X, y, z))


def from_z(block, distance):
    return permuted(block, lambda grp, x, y, z: (grp, x, y, (z - distance) % N_Z))


def unit_rows(values):
    return (values / jnp.sqrt(jnp.sum(values * values, -1, keepdims=True) + EPS)).astype(
        jnp.bfloat16
    )


def diagonal():
    return lax.broadcasted_iota(jnp.int32, (128, 128), 0) == lax.broadcasted_iota(
        jnp.int32, (128, 128), 1
    )


def to_row(column):
    return jnp.sum(jnp.where(diagonal(), column, 0.0), axis=0, keepdims=True)


def to_column(row):
    return jnp.sum(jnp.where(diagonal(), row, 0.0), axis=1, keepdims=True)


def lanes(pieces):
    return jnp.concatenate([pieces[k : k + 1, :] for k in range(pieces.shape[0])], axis=1)


def pieces_of(row):
    return jnp.concatenate([row[:, k * 128 : (k + 1) * 128] for k in range(8)], axis=0)


def unit_kernel(
    place_ref,
    features_ref,
    other_features_ref,
    mask_ref,
    own_ref,
    other_ref,
    pack_ref,
    weight_ref,
    unit_ref,
    other_unit_ref,
):
    grp, x = place_ref[0], place_ref[1]

    @pl.when(pl.program_id(0) == 0)
    def _():
        own = unit_rows(features_ref[...].astype(jnp.float32))
        other = unit_rows(other_features_ref[...].astype(jnp.float32))
        teacher = jnp.where(grp == 0, other, own)
        student = jnp.where(grp == 0, own, other)
        crop = mask_ref[pl.ds(x % 2 * 2, 2), :].astype(jnp.float32)
        count = jnp.maximum(jnp.sum(crop), 1.0)
        weight = mask_ref[pl.ds(x % 2 * 2 + grp, 1), :].astype(jnp.float32)
        weight = weight / (STUDENT_TEMP * count)
        weight_ref[...] = jnp.broadcast_to(weight, (8, 128)).astype(jnp.bfloat16)
        pack_ref[0:OWN_ROWS, :] = teacher
        pack_ref[OWN_ROWS:PACK, :] = student

    own, other = own_ref[...], other_ref[...]
    student = jnp.where(grp == 0, own, other)
    blended = MOMENTUM * jnp.where(grp == 0, other, own) + (1.0 - MOMENTUM) * student
    student, blended = unit_rows(student), unit_rows(blended)
    unit_ref[...] = jnp.where(grp == 0, student, blended)
    other_unit_ref[...] = jnp.where(grp == 0, blended, student)


def in_hbm(array):
    return pltpu.with_memory_space_constraint(array, pltpu.HBM)


def unit_call(place, features, other_features, mask, own_master, other_master):
    rows = BLOCK // 2
    picked = pl.BlockSpec((OWN_ROWS, 256), lambda i, place: (place[1] % 2 * 2 + place[0], 0))
    part = pl.BlockSpec((rows, 256), lambda i, place: (i, 0))
    return pl.pallas_call(
        unit_kernel,
        out_shape=[
            shape((PACK, 256), jnp.bfloat16),
            shape((8, 128), jnp.bfloat16),
            shape((BLOCK, 256), jnp.bfloat16),
            shape((BLOCK, 256), jnp.bfloat16),
        ],
        grid_spec=pltpu.PrefetchScalarGridSpec(
            num_scalar_prefetch=1,
            grid=(2,),
            in_specs=[
                picked,
                picked,
                pl.BlockSpec((4, 128), lambda i, place: (0, 0)),
                part,
                part,
            ],
            out_specs=[
                pl.BlockSpec((PACK, 256), lambda i, place: (0, 0)),
                pl.BlockSpec((8, 128), lambda i, place: (0, 0)),
                part,
                part,
            ],
        ),
        compiler_params=pltpu.CompilerParams(vmem_limit_bytes=VMEM_LIMIT),
    )(place, in_hbm(features), other_features, in_hbm(mask), in_hbm(own_master), other_master)


def exp_of(protos, tokens, temperature):
    logits = lax.dot_general(
        protos, tokens, (((1,), (1,)), ((), ())), preferred_element_type=jnp.float32
    )
    return jnp.exp2(logits * (LOG2E / temperature))


def exp_kernel(*refs):
    place_ref, pack_refs = refs[0], refs[1:9]
    own_refs, other_refs = refs[9:13], refs[13:17]
    teacher_ref, student_ref, parts_ref, total_ref, token_ref = refs[17:22]
    scratch_ref, vector_ref = refs[22:]
    grp, x, z = place_ref[0], place_ref[1], place_ref[2]
    for k in range(N_Z):
        rows = pl.ds(pl.multiple_of((z + k) % N_Z * OWN_ROWS, OWN_ROWS), OWN_ROWS)
        scratch_ref[rows, :] = pack_refs[k][0:OWN_ROWS, :]
        token_ref[rows, :] = pack_refs[k][OWN_ROWS:PACK, :]
    teacher_tokens = scratch_ref[...]
    student_tokens = token_ref[...]
    total = jnp.zeros((8, ROWS), jnp.float32)
    for k in range(N_X):
        base = (x + k) % N_X * BLOCK
        for i in range(BLOCK // 256):
            block = slice(i * 256, (i + 1) * 256)
            rows = pl.ds(pl.multiple_of(base + i * 256, 256), 256)
            own, other = own_refs[k][block, :], other_refs[k][block, :]
            values = exp_of(jnp.where(grp == 0, other, own), teacher_tokens, TEACHER_TEMP)
            teacher_ref[rows, :] = values
            folded = sum(values[:, k * 128 : (k + 1) * 128] for k in range(8))
            column = jnp.sum(folded, axis=1, keepdims=True)
            for h in range(2):
                vector_ref[pl.ds(base // 128 + i * 2 + h, 1), :] = to_row(
                    column[h * 128 : (h + 1) * 128]
                )
            values = exp_of(jnp.where(grp == 0, own, other), student_tokens, STUDENT_TEMP)
            student_ref[rows, :] = values
            total += jnp.sum(values.reshape(32, 8, ROWS), axis=0)
    total_ref[...] = pieces_of(jnp.sum(total, axis=0, keepdims=True))
    for k in range(N_COLGRP):
        parts_ref[k] = vector_ref[...]


def row_kernel(with_extra, *refs):
    if with_extra:
        parts_ref, exp_ref, extra_ref, out_ref, scale_ref = refs
    else:
        parts_ref, exp_ref, out_ref, scale_ref = refs
    scale = 1.0 / jnp.sum(parts_ref[...], axis=0)
    scale_ref[...] = scale
    total = jnp.zeros((8, ROWS), jnp.float32)
    for j in range(COLS // 128):
        weighted = exp_ref[j * 128 : (j + 1) * 128, :] * to_column(scale[j : j + 1, :])
        total += jnp.sum(weighted.reshape(16, 8, ROWS), axis=0)
    mine = pieces_of(jnp.sum(total, axis=0, keepdims=True))
    if with_extra:
        mine = jnp.concatenate([mine, extra_ref[...].astype(jnp.float32)], axis=0)
    mine = mine.astype(jnp.bfloat16)
    for k in range(N_ROWGRP):
        out_ref[k] = mine


def col_kernel(with_weight, *refs):
    if with_weight:
        parts_ref, exp_ref, out_ref, weight_ref, vector_ref = refs
        for z in range(N_Z):
            extra = parts_ref[z * N_Y, 8:16, :].astype(jnp.float32)
            weight_ref[z : z + 1, :] = extra[0:1, :]
    else:
        parts_ref, exp_ref, out_ref, vector_ref = refs
    row = lanes(1.0 / jnp.sum(parts_ref[:, 0:8, :].astype(jnp.float32), axis=0))
    for j in range(COLS // 128):
        weighted = exp_ref[j * 128 : (j + 1) * 128, :] * row
        folded = sum(weighted[:, k * 128 : (k + 1) * 128] for k in range(8))
        vector_ref[j : j + 1, :] = to_row(jnp.sum(folded, axis=1, keepdims=True))
    for k in range(N_COLGRP):
        out_ref[k] = vector_ref[...]


def grad_kernel(
    other,
    pieces,
    place_ref,
    parts_ref,
    scale_ref,
    weight_ref,
    teacher_exp_ref,
    student_exp_ref,
    token_ref,
    out_ref,
):
    inverse = 1.0 / jnp.sum(parts_ref[...].astype(jnp.float32), axis=0)
    row_inverse, student_inverse = lanes(inverse[0:8, :]), lanes(inverse[8:16, :])
    weight = lanes(weight_ref[...] * PROTOS)
    teacher_row, student_row = row_inverse * weight, student_inverse * weight
    first = 1 - place_ref[0] if other else place_ref[0]
    for n, k in enumerate(pieces):
        base = (place_ref[1] + 2 * k + first) % N_X * BLOCK
        for i in range(BLOCK // 256):
            errors = []
            for h in range(2):
                start = base + i * 256 + h * 128
                column = to_column(scale_ref[pl.ds(start // 128, 1), :])
                rows = pl.ds(pl.multiple_of(start, 128), 128)
                targets = teacher_exp_ref[rows, :] * column * teacher_row
                probs = student_exp_ref[rows, :] * student_row
                errors.append((probs - targets).astype(jnp.bfloat16))
            out_ref[n, i * 256 : (i + 1) * 256, :] = jnp.dot(
                jnp.concatenate(errors, axis=0),
                token_ref[...],
                preferred_element_type=jnp.float32,
            ).astype(out_ref.dtype)


def call(kernel, outs, scratch, *args, flops=0, transcendentals=0):
    vmem = pl.BlockSpec(memory_space=pltpu.VMEM)
    smem = pl.BlockSpec(memory_space=pltpu.SMEM)
    return pl.pallas_call(
        kernel,
        out_shape=outs,
        in_specs=[smem if a.ndim == 1 else vmem for a in args],
        out_specs=[vmem] * len(outs),
        scratch_shapes=scratch,
        compiler_params=pltpu.CompilerParams(vmem_limit_bytes=VMEM_LIMIT),
        cost_estimate=pl.CostEstimate(
            flops=flops, transcendentals=transcendentals, bytes_accessed=COLS * ROWS * 4
        ),
    )(*args)


def shape(dims, dtype=jnp.float32):
    return jax.ShapeDtypeStruct(dims, dtype)


def per_device(features, masters, patch_mask):
    grp = lax.axis_index("grp")
    x = lax.axis_index("img") // N_Z * 2 + lax.axis_index("tp") // N_Y
    z = lax.axis_index("img") % N_Z
    place = jnp.stack([grp, x, z]).astype(jnp.int32)
    work = COLS * ROWS

    own_master = masters[0]
    other_master = swapped(own_master)
    other_features = swapped(features[0])
    pack, weight, unit, other_unit = unit_call(
        place,
        features[0],
        other_features,
        patch_mask.reshape(4, 128),
        own_master,
        other_master,
    )
    packs = {0: pack}
    for k in range(1, 5):
        packs[k] = from_z(packs[k - 1], 1)
        if k < 4:
            packs[N_Z - k] = from_z(packs[(N_Z - k + 1) % N_Z], -1)
    own_units = [unit, from_x(unit, 1), None, from_x(unit, -1)]
    own_units[2] = from_x(own_units[1], 1)
    near, _ = lax.optimization_barrier(((own_units[1], own_units[3]), (packs[3], packs[5])))
    far, packs = lax.optimization_barrier((own_units[2], packs))
    other_units = [other_unit, swapped(near[0]), swapped(far), swapped(near[1])]

    teacher_exp, student_exp, col_parts, student_part, student_tokens = call(
        exp_kernel,
        [
            shape((COLS, ROWS)),
            shape((COLS, ROWS)),
            shape((N_COLGRP, 16, 128)),
            shape((8, 128)),
            shape((ROWS, 256), jnp.bfloat16),
        ],
        [pltpu.VMEM((ROWS, 256), jnp.bfloat16), pltpu.VMEM((16, 128), jnp.float32)],
        place,
        *(packs[k] for k in range(N_Z)),
        *own_units,
        *other_units,
        flops=4 * work * 256,
        transcendentals=2 * work,
    )

    for sweep in range(3):
        first, last = sweep == 0, sweep == 2
        extra = (weight,) if first else (student_part,) if last else ()
        col_parts = exchange(col_parts, COL_GROUPS)
        row_parts, col_scale = call(
            functools.partial(row_kernel, first or last),
            [shape((N_ROWGRP, 16 if extra else 8, 128), jnp.bfloat16), shape((16, 128))],
            [],
            col_parts,
            teacher_exp,
            *extra,
            flops=2 * work,
        )
        row_parts = exchange(row_parts, ROW_GROUPS)
        if not last:
            col_parts, *rest = call(
                functools.partial(col_kernel, first),
                [shape((N_COLGRP, 16, 128))] + [shape((8, 128))] * first,
                [pltpu.VMEM((16, 128), jnp.float32)],
                row_parts,
                teacher_exp,
                flops=2 * work,
            )
            if first:
                (weights,) = rest

    def partial_gradient(other, pieces, dtype):
        (out,) = call(
            functools.partial(grad_kernel, other, pieces),
            [shape((len(pieces), BLOCK, 256), dtype)],
            [],
            place,
            row_parts,
            col_scale,
            weights,
            teacher_exp,
            student_exp,
            student_tokens,
            flops=work * 256,
        )
        return out

    received = swapped(partial_gradient(True, (0, 1), jnp.bfloat16))
    chip = partial_gradient(False, (0, 1), jnp.float32) + received.astype(jnp.float32)
    near, far = chip[0].astype(jnp.bfloat16), chip[1].astype(jnp.bfloat16)

    def sent(block, source, distance):
        return permuted(
            block,
            lambda grp, x, y, z: (0, (x + distance) % N_X, y, z) if grp == source else None,
        ).astype(jnp.float32)

    gradient = chip[0] + sent(far, 0, 2) + sent(near, 1, 1) + sent(far, 1, 3)
    blended = MOMENTUM * own_master + (1.0 - MOMENTUM) * other_master
    return jnp.where(grp == 1, blended, gradient)[None]


def solution(mesh):
    in_specs = (P("grp", "img", None), P("grp", ("img", "tp"), None), P("img"))
    out_specs = P("grp", ("img", "tp"), None)
    return jax.shard_map(
        per_device, mesh=mesh, in_specs=in_specs, out_specs=out_specs, check_vma=False
    )
```

```python
import functools

import jax
import jax.numpy as jnp
from jax import lax
from jax.experimental import pallas as pl
from jax.experimental.pallas import tpu as pltpu
from jax.sharding import PartitionSpec as P

PROTOS = 65536
PATCHES = 256
MOMENTUM = 0.994
TEACHER_TEMP = 0.07
STUDENT_TEMP = 0.1
EPS = 1e-06
LOG2E = 1.4426950408889634

AXES = ("grp", "img", "tp")
N_GRP, N_IMG, N_TP = 2, 16, 8
N_X, N_Y, N_Z = 4, 4, 8
BLOCK = 512
HALF = 256
STEP = 512
OWN_ROWS = 128
PACK = 2 * OWN_ROWS
ROWS = N_Z * OWN_ROWS
COLS = N_X * BLOCK
N_ROWGRP = N_Y * N_Z
N_COLGRP = N_GRP * N_X
VMEM_LIMIT = 16 * 1024 * 1024


def coordinates(device):
    grp, rest = divmod(device, N_IMG * N_TP)
    img, tp = divmod(rest, N_TP)
    x_hi, z = divmod(img, N_Z)
    x_lo, y = divmod(tp, N_Y)
    return grp, x_hi * 2 + x_lo, y, z


def device_at(grp, x, y, z):
    return ((grp * 2 + x // 2) * N_Z + z) * N_TP + x % 2 * N_Y + y


def groups_of(key):
    found = {}
    for device in range(N_GRP * N_IMG * N_TP):
        found.setdefault(key(*coordinates(device)), []).append(device)
    return list(found.values())


COL_GROUPS = groups_of(lambda grp, x, y, z: (y, z))
ROW_GROUPS = groups_of(lambda grp, x, y, z: (grp, x))


def exchange(blocks, groups):
    return lax.all_to_all(blocks, AXES, 0, 0, axis_index_groups=groups, tiled=True)


def swapped(block):
    return lax.ppermute(block, "grp", [(0, 1), (1, 0)])


def permuted(block, target_of):
    route = []
    for device in range(N_GRP * N_IMG * N_TP):
        target = target_of(*coordinates(device))
        if target is not None:
            route.append((device, device_at(*target)))
    return lax.ppermute(block, AXES, route)


def from_x(block, distance):
    return permuted(block, lambda grp, x, y, z: (grp, (x - distance) % N_X, y, z))


def from_z(block, distance):
    return permuted(block, lambda grp, x, y, z: (grp, x, y, (z - distance) % N_Z))


def unit_rows(values):
    return (values / jnp.sqrt(jnp.sum(values * values, -1, keepdims=True) + EPS)).astype(
        jnp.bfloat16
    )


def diagonal():
    return lax.broadcasted_iota(jnp.int32, (128, 128), 0) == lax.broadcasted_iota(
        jnp.int32, (128, 128), 1
    )


def to_row(column):
    return jnp.sum(jnp.where(diagonal(), column, 0.0), axis=0, keepdims=True)


def to_column(row):
    return jnp.sum(jnp.where(diagonal(), row, 0.0), axis=1, keepdims=True)


def lanes(pieces):
    return jnp.concatenate([pieces[k : k + 1, :] for k in range(pieces.shape[0])], axis=1)


def pieces_of(row):
    return jnp.concatenate([row[:, k * 128 : (k + 1) * 128] for k in range(8)], axis=0)


def unit_kernel(
    place_ref,
    features_ref,
    other_features_ref,
    mask_ref,
    own_ref,
    other_ref,
    pack_ref,
    weight_ref,
    unit_ref,
    other_unit_ref,
):
    grp, x = place_ref[0], place_ref[1]

    @pl.when(pl.program_id(0) == 0)
    def _():
        own = unit_rows(features_ref[...].astype(jnp.float32))
        other = unit_rows(other_features_ref[...].astype(jnp.float32))
        teacher = jnp.where(grp == 0, other, own)
        student = jnp.where(grp == 0, own, other)
        crop = mask_ref[pl.ds(x % 2 * 2, 2), :].astype(jnp.float32)
        count = jnp.maximum(jnp.sum(crop), 1.0)
        weight = mask_ref[pl.ds(x % 2 * 2 + grp, 1), :].astype(jnp.float32)
        weight = weight / (STUDENT_TEMP * count)
        weight_ref[...] = jnp.broadcast_to(weight, (8, 128)).astype(jnp.bfloat16)
        pack_ref[0:OWN_ROWS, :] = teacher
        pack_ref[OWN_ROWS:PACK, :] = student

    own, other = own_ref[...], other_ref[...]
    student = jnp.where(grp == 0, own, other)
    blended = MOMENTUM * jnp.where(grp == 0, other, own) + (1.0 - MOMENTUM) * student
    student, blended = unit_rows(student), unit_rows(blended)
    unit_ref[...] = jnp.where(grp == 0, student, blended)
    other_unit_ref[...] = jnp.where(grp == 0, blended, student)


def in_hbm(array):
    return pltpu.with_memory_space_constraint(array, pltpu.HBM)


def unit_call(place, features, other_features, mask, own_master, other_master):
    rows = BLOCK // 2
    picked = pl.BlockSpec((OWN_ROWS, 256), lambda i, place: (place[1] % 2 * 2 + place[0], 0))
    part = pl.BlockSpec((rows, 256), lambda i, place: (i, 0))
    return pl.pallas_call(
        unit_kernel,
        out_shape=[
            shape((PACK, 256), jnp.bfloat16),
            shape((8, 128), jnp.bfloat16),
            shape((BLOCK, 256), jnp.bfloat16),
            shape((BLOCK, 256), jnp.bfloat16),
        ],
        grid_spec=pltpu.PrefetchScalarGridSpec(
            num_scalar_prefetch=1,
            grid=(2,),
            in_specs=[
                picked,
                picked,
                pl.BlockSpec((4, 128), lambda i, place: (0, 0)),
                part,
                part,
            ],
            out_specs=[
                pl.BlockSpec((PACK, 256), lambda i, place: (0, 0)),
                pl.BlockSpec((8, 128), lambda i, place: (0, 0)),
                part,
                part,
            ],
        ),
        compiler_params=pltpu.CompilerParams(vmem_limit_bytes=VMEM_LIMIT),
    )(place, in_hbm(features), other_features, in_hbm(mask), in_hbm(own_master), other_master)


def exp_of(protos, tokens, temperature):
    logits = lax.dot_general(
        protos, tokens, (((1,), (1,)), ((), ())), preferred_element_type=jnp.float32
    )
    return jnp.exp2(logits * (LOG2E / temperature))


def exp_kernel(chunks, resumed, *refs):
    place_ref, pack_refs = refs[0], refs[1 : 1 + len(chunks)]
    refs = refs[1 + len(chunks) :]
    own_refs, other_refs, refs = refs[0:4], refs[4:8], refs[8:]
    if resumed:
        sums_ref, refs = refs[0], refs[5:]
    parts_ref, teacher_ref, student_ref, total_ref, token_ref, scratch_ref = refs
    grp, x, z = place_ref[0], place_ref[1], place_ref[2]
    places = [(z + k) % N_Z for k in chunks]
    pairs = range(len(chunks) // 2)
    for n, place in enumerate(places):
        scratch_ref[n * OWN_ROWS : (n + 1) * OWN_ROWS, :] = pack_refs[n][0:OWN_ROWS, :]
        rows = pl.ds(pl.multiple_of(place * OWN_ROWS, OWN_ROWS), OWN_ROWS)
        token_ref[rows, :] = pack_refs[n][OWN_ROWS:PACK, :]
    totals = [jnp.zeros((8, 128), jnp.float32) for _ in chunks]
    for k in range(N_X):
        base = (x + k) % N_X * BLOCK
        for i in range(BLOCK // STEP):
            block = slice(i * STEP, (i + 1) * STEP)
            rows = pl.ds(pl.multiple_of(base + i * STEP, STEP), STEP)
            own, other = own_refs[k][block, :], other_refs[k][block, :]
            teacher, student = jnp.where(grp == 0, other, own), jnp.where(grp == 0, own, other)
            folded = jnp.zeros((STEP, 128), jnp.float32)
            for p in pairs:
                tokens = scratch_ref[p * 256 : (p + 1) * 256, :]
                values = exp_of(teacher, tokens, TEACHER_TEMP)
                tokens = jnp.concatenate(
                    [pack_refs[2 * p + h][OWN_ROWS:PACK, :] for h in range(2)], axis=0
                )
                others = exp_of(student, tokens, STUDENT_TEMP)
                for h in range(2):
                    n = 2 * p + h
                    half = values[:, h * 128 : (h + 1) * 128]
                    teacher_ref[places[n], rows, :] = half
                    folded += half
                    half = others[:, h * 128 : (h + 1) * 128]
                    student_ref[places[n], rows, :] = half
                    totals[n] += jnp.sum(half.reshape(STEP // 8, 8, 128), axis=0)
            column = jnp.sum(folded, axis=1, keepdims=True)
            for h in range(STEP // 128):
                line = pl.ds(base // 128 + i * (STEP // 128) + h, 1)
                sums = to_row(column[h * 128 : (h + 1) * 128])
                if resumed:
                    sums += sums_ref[line, :]
                    for target in range(N_COLGRP):
                        parts_ref[target, line, :] = sums
                else:
                    parts_ref[line, :] = sums
    for n, place in enumerate(places):
        total_ref[pl.ds(place, 1), :] = jnp.sum(totals[n], axis=0, keepdims=True)


def row_kernel(with_extra, *refs):
    if with_extra:
        parts_ref, exp_ref, extra_ref, out_ref, scale_ref = refs
    else:
        parts_ref, exp_ref, out_ref, scale_ref = refs
    scale = 1.0 / jnp.sum(parts_ref[...], axis=0)
    scale_ref[...] = scale
    totals = [jnp.zeros((8, 128), jnp.float32) for _ in range(N_Z)]
    for j in range(COLS // 128):
        column = to_column(scale[j : j + 1, :])
        for k in range(N_Z):
            weighted = exp_ref[k, j * 128 : (j + 1) * 128, :] * column
            totals[k] += jnp.sum(weighted.reshape(16, 8, 128), axis=0)
    mine = jnp.concatenate([jnp.sum(t, axis=0, keepdims=True) for t in totals], axis=0)
    if with_extra:
        mine = jnp.concatenate([mine, extra_ref[...].astype(jnp.float32)], axis=0)
    mine = mine.astype(jnp.bfloat16)
    for k in range(N_ROWGRP):
        out_ref[k] = mine


def col_kernel(with_weight, *refs):
    if with_weight:
        parts_ref, exp_ref, out_ref, weight_ref, vector_ref = refs
        for z in range(N_Z):
            extra = parts_ref[z * N_Y, 8:16, :].astype(jnp.float32)
            weight_ref[z : z + 1, :] = extra[0:1, :]
    else:
        parts_ref, exp_ref, out_ref, vector_ref = refs
    scale = 1.0 / jnp.sum(parts_ref[:, 0:8, :].astype(jnp.float32), axis=0)
    for j in range(COLS // 128):
        rows = slice(j * 128, (j + 1) * 128)
        folded = sum(exp_ref[k, rows, :] * scale[k : k + 1, :] for k in range(N_Z))
        vector_ref[j : j + 1, :] = to_row(jnp.sum(folded, axis=1, keepdims=True))
    for k in range(N_COLGRP):
        out_ref[k] = vector_ref[...]


def grad_kernel(
    other,
    pieces,
    place_ref,
    parts_ref,
    scale_ref,
    weight_ref,
    teacher_exp_ref,
    student_exp_ref,
    token_ref,
    out_ref,
):
    inverse = 1.0 / jnp.sum(parts_ref[...].astype(jnp.float32), axis=0)
    weight = weight_ref[...] * PROTOS
    teacher_row, student_row = inverse[0:8, :] * weight, inverse[8:16, :] * weight
    first = 1 - place_ref[0] if other else place_ref[0]
    for n, k in enumerate(pieces):
        base = (place_ref[1] + 2 * k + first) % N_X * BLOCK
        for i in range(BLOCK // 256):
            errors = []
            for h in range(2):
                start = base + i * 256 + h * 128
                column = to_column(scale_ref[pl.ds(start // 128, 1), :])
                rows = pl.ds(pl.multiple_of(start, 128), 128)
                line = []
                for z in range(N_Z):
                    targets = teacher_exp_ref[z, rows, :] * column * teacher_row[z : z + 1, :]
                    probs = student_exp_ref[z, rows, :] * student_row[z : z + 1, :]
                    line.append((probs - targets).astype(jnp.bfloat16))
                errors.append(jnp.concatenate(line, axis=1))
            out_ref[n, i * 256 : (i + 1) * 256, :] = jnp.dot(
                jnp.concatenate(errors, axis=0),
                token_ref[...],
                preferred_element_type=jnp.float32,
            ).astype(out_ref.dtype)


def call(kernel, outs, scratch, *args, flops=0, transcendentals=0, aliases=None):
    vmem = pl.BlockSpec(memory_space=pltpu.VMEM)
    smem = pl.BlockSpec(memory_space=pltpu.SMEM)
    return pl.pallas_call(
        kernel,
        out_shape=outs,
        in_specs=[smem if a.ndim == 1 else vmem for a in args],
        out_specs=[vmem] * len(outs),
        scratch_shapes=scratch,
        input_output_aliases=aliases or {},
        compiler_params=pltpu.CompilerParams(vmem_limit_bytes=VMEM_LIMIT),
        cost_estimate=pl.CostEstimate(
            flops=flops, transcendentals=transcendentals, bytes_accessed=COLS * ROWS * 4
        ),
    )(*args)


def shape(dims, dtype=jnp.float32):
    return jax.ShapeDtypeStruct(dims, dtype)


def per_device(features, masters, patch_mask):
    grp = lax.axis_index("grp")
    x = lax.axis_index("img") // N_Z * 2 + lax.axis_index("tp") // N_Y
    z = lax.axis_index("img") % N_Z
    place = jnp.stack([grp, x, z]).astype(jnp.int32)
    work = COLS * ROWS

    own_master = masters[0]
    other_master = swapped(own_master)
    other_features = swapped(features[0])
    pack, weight, unit, other_unit = unit_call(
        place,
        features[0],
        other_features,
        patch_mask.reshape(4, 128),
        own_master,
        other_master,
    )
    packs = {0: pack}
    for k in range(1, 5):
        packs[k] = from_z(packs[k - 1], 1)
        if k < 4:
            packs[N_Z - k] = from_z(packs[(N_Z - k + 1) % N_Z], -1)
    own_units = [unit, from_x(unit, 1), None, from_x(unit, -1)]
    own_units[2] = from_x(own_units[1], 1)
    near, _ = lax.optimization_barrier((tuple(own_units[1:]), (packs[3], packs[5])))
    other_units = [other_unit] + [swapped(block) for block in near]

    held = [
        shape((N_Z, COLS, 128)),
        shape((N_Z, COLS, 128)),
        shape((8, 128)),
        shape((ROWS, 256), jnp.bfloat16),
    ]

    def exponents(chunks, first_out, aliases, *carried):
        return call(
            functools.partial(exp_kernel, chunks, bool(carried)),
            [first_out] + held,
            [pltpu.VMEM((len(chunks) * OWN_ROWS, 256), jnp.bfloat16)],
            place,
            *(packs[k] for k in chunks),
            *own_units,
            *other_units,
            *carried,
            flops=len(chunks) * work * 256 // 2,
            transcendentals=len(chunks) * work // 4,
            aliases=aliases,
        )

    early, late = (0, 1, 7, 2, 6, 3), (5, 4)
    carried = exponents(early, shape((16, 128)), None)
    start = 1 + len(late) + 2 * N_X + 1
    col_parts, teacher_exp, student_exp, student_part, student_tokens = exponents(
        late,
        shape((N_COLGRP, 16, 128)),
        {start + n: 1 + n for n in range(4)},
        *carried,
    )

    for sweep in range(3):
        first, last = sweep == 0, sweep == 2
        extra = (weight,) if first else (student_part,) if last else ()
        col_parts = exchange(col_parts, COL_GROUPS)
        row_parts, col_scale = call(
            functools.partial(row_kernel, first or last),
            [shape((N_ROWGRP, 16 if extra else 8, 128), jnp.bfloat16), shape((16, 128))],
            [],
            col_parts,
            teacher_exp,
            *extra,
            flops=2 * work,
        )
        row_parts = exchange(row_parts, ROW_GROUPS)
        if not last:
            col_parts, *rest = call(
                functools.partial(col_kernel, first),
                [shape((N_COLGRP, 16, 128))] + [shape((8, 128))] * first,
                [pltpu.VMEM((16, 128), jnp.float32)],
                row_parts,
                teacher_exp,
                flops=2 * work,
            )
            if first:
                (weights,) = rest

    def partial_gradient(other, pieces, dtype):
        (out,) = call(
            functools.partial(grad_kernel, other, pieces),
            [shape((len(pieces), BLOCK, 256), dtype)],
            [],
            place,
            row_parts,
            col_scale,
            weights,
            teacher_exp,
            student_exp,
            student_tokens,
            flops=work * 256,
        )
        return out

    received = swapped(partial_gradient(True, (0, 1), jnp.bfloat16))
    chip = partial_gradient(False, (0, 1), jnp.float32) + received.astype(jnp.float32)
    near, far = chip[0].astype(jnp.bfloat16), chip[1].astype(jnp.bfloat16)

    def sent(block, source, distance):
        return permuted(
            block,
            lambda grp, x, y, z: (0, (x + distance) % N_X, y, z) if grp == source else None,
        ).astype(jnp.float32)

    gradient = chip[0] + sent(far, 0, 2) + sent(near, 1, 1) + sent(far, 1, 3)
    blended = MOMENTUM * own_master + (1.0 - MOMENTUM) * other_master
    return jnp.where(grp == 1, blended, gradient)[None]


def solution(mesh):
    in_specs = (P("grp", "img", None), P("grp", ("img", "tp"), None), P("img"))
    out_specs = P("grp", ("img", "tp"), None)
    return jax.shard_map(
        per_device, mesh=mesh, in_specs=in_specs, out_specs=out_specs, check_vma=False
    )
```

```python
import functools

import jax
import jax.numpy as jnp
from jax import lax
from jax.experimental import pallas as pl
from jax.experimental.pallas import tpu as pltpu
from jax.sharding import PartitionSpec as P

PROTOS = 65536
PATCHES = 256
MOMENTUM = 0.994
TEACHER_TEMP = 0.07
STUDENT_TEMP = 0.1
EPS = 1e-06
LOG2E = 1.4426950408889634

AXES = ("grp", "img", "tp")
N_GRP, N_IMG, N_TP = 2, 16, 8
N_X, N_Y, N_Z = 4, 4, 8
BLOCK = 512
HALF = 256
STEP = 512
OWN_ROWS = 128
PACK = 2 * OWN_ROWS
ROWS = N_Z * OWN_ROWS
COLS = N_X * BLOCK
N_ROWGRP = N_Y * N_Z
N_COLGRP = N_GRP * N_X
VMEM_LIMIT = 16 * 1024 * 1024


def coordinates(device):
    grp, rest = divmod(device, N_IMG * N_TP)
    img, tp = divmod(rest, N_TP)
    x_hi, z = divmod(img, N_Z)
    x_lo, y = divmod(tp, N_Y)
    return grp, x_hi * 2 + x_lo, y, z


def device_at(grp, x, y, z):
    return ((grp * 2 + x // 2) * N_Z + z) * N_TP + x % 2 * N_Y + y


def groups_of(key):
    found = {}
    for device in range(N_GRP * N_IMG * N_TP):
        found.setdefault(key(*coordinates(device)), []).append(device)
    return list(found.values())


COL_GROUPS = groups_of(lambda grp, x, y, z: (y, z))
ROW_GROUPS = groups_of(lambda grp, x, y, z: (grp, x))


def exchange(blocks, groups):
    return lax.all_to_all(blocks, AXES, 0, 0, axis_index_groups=groups, tiled=True)


def swapped(block):
    return lax.ppermute(block, "grp", [(0, 1), (1, 0)])


def permuted(block, target_of):
    route = []
    for device in range(N_GRP * N_IMG * N_TP):
        target = target_of(*coordinates(device))
        if target is not None:
            route.append((device, device_at(*target)))
    return lax.ppermute(block, AXES, route)


def from_x(block, distance):
    return permuted(block, lambda grp, x, y, z: (grp, (x - distance) % N_X, y, z))


def from_z(block, distance):
    return permuted(block, lambda grp, x, y, z: (grp, x, y, (z - distance) % N_Z))


def unit_rows(values):
    return (values / jnp.sqrt(jnp.sum(values * values, -1, keepdims=True) + EPS)).astype(
        jnp.bfloat16
    )


def diagonal():
    return lax.broadcasted_iota(jnp.int32, (128, 128), 0) == lax.broadcasted_iota(
        jnp.int32, (128, 128), 1
    )


def to_row(column):
    return jnp.sum(jnp.where(diagonal(), column, 0.0), axis=0, keepdims=True)


def to_column(row):
    return jnp.sum(jnp.where(diagonal(), row, 0.0), axis=1, keepdims=True)


def lanes(pieces):
    return jnp.concatenate([pieces[k : k + 1, :] for k in range(pieces.shape[0])], axis=1)


def pieces_of(row):
    return jnp.concatenate([row[:, k * 128 : (k + 1) * 128] for k in range(8)], axis=0)


def unit_kernel(
    place_ref,
    features_ref,
    other_features_ref,
    mask_ref,
    own_ref,
    other_ref,
    pack_ref,
    weight_ref,
    unit_ref,
    other_unit_ref,
):
    grp, x = place_ref[0], place_ref[1]

    @pl.when(pl.program_id(0) == 0)
    def _():
        own = unit_rows(features_ref[...].astype(jnp.float32))
        other = unit_rows(other_features_ref[...].astype(jnp.float32))
        teacher = jnp.where(grp == 0, other, own)
        student = jnp.where(grp == 0, own, other)
        crop = mask_ref[pl.ds(x % 2 * 2, 2), :].astype(jnp.float32)
        count = jnp.maximum(jnp.sum(crop), 1.0)
        weight = mask_ref[pl.ds(x % 2 * 2 + grp, 1), :].astype(jnp.float32)
        weight = weight / (STUDENT_TEMP * count)
        weight_ref[...] = jnp.broadcast_to(weight, (8, 128)).astype(jnp.bfloat16)
        pack_ref[0:OWN_ROWS, :] = teacher
        pack_ref[OWN_ROWS:PACK, :] = student

    own, other = own_ref[...], other_ref[...]
    student = jnp.where(grp == 0, own, other)
    blended = MOMENTUM * jnp.where(grp == 0, other, own) + (1.0 - MOMENTUM) * student
    student, blended = unit_rows(student), unit_rows(blended)
    unit_ref[...] = jnp.where(grp == 0, student, blended)
    other_unit_ref[...] = jnp.where(grp == 0, blended, student)


def in_hbm(array):
    return pltpu.with_memory_space_constraint(array, pltpu.HBM)


def unit_call(place, features, other_features, mask, own_master, other_master):
    rows = BLOCK // 2
    picked = pl.BlockSpec((OWN_ROWS, 256), lambda i, place: (place[1] % 2 * 2 + place[0], 0))
    part = pl.BlockSpec((rows, 256), lambda i, place: (i, 0))
    return pl.pallas_call(
        unit_kernel,
        out_shape=[
            shape((PACK, 256), jnp.bfloat16),
            shape((8, 128), jnp.bfloat16),
            shape((BLOCK, 256), jnp.bfloat16),
            shape((BLOCK, 256), jnp.bfloat16),
        ],
        grid_spec=pltpu.PrefetchScalarGridSpec(
            num_scalar_prefetch=1,
            grid=(2,),
            in_specs=[
                picked,
                picked,
                pl.BlockSpec((4, 128), lambda i, place: (0, 0)),
                part,
                part,
            ],
            out_specs=[
                pl.BlockSpec((PACK, 256), lambda i, place: (0, 0)),
                pl.BlockSpec((8, 128), lambda i, place: (0, 0)),
                part,
                part,
            ],
        ),
        compiler_params=pltpu.CompilerParams(vmem_limit_bytes=VMEM_LIMIT),
    )(place, in_hbm(features), other_features, in_hbm(mask), in_hbm(own_master), other_master)


def exp_of(protos, tokens, temperature):
    logits = lax.dot_general(
        protos, tokens, (((1,), (1,)), ((), ())), preferred_element_type=jnp.float32
    )
    return jnp.exp2(logits * (LOG2E / temperature))


def exp_kernel(chunks, resumed, *refs):
    place_ref, pack_refs = refs[0], refs[1 : 1 + len(chunks)]
    refs = refs[1 + len(chunks) :]
    own_refs, other_refs, refs = refs[0:4], refs[4:8], refs[8:]
    if resumed:
        sums_ref, refs = refs[0], refs[5:]
    parts_ref, teacher_ref, student_ref, total_ref, token_ref, scratch_ref = refs
    grp, x, z = place_ref[0], place_ref[1], place_ref[2]
    places = [(z + k) % N_Z for k in chunks]
    pairs = range(len(chunks) // 2)
    for n, place in enumerate(places):
        scratch_ref[n * OWN_ROWS : (n + 1) * OWN_ROWS, :] = pack_refs[n][0:OWN_ROWS, :]
        rows = pl.ds(pl.multiple_of(place * OWN_ROWS, OWN_ROWS), OWN_ROWS)
        token_ref[rows, :] = pack_refs[n][OWN_ROWS:PACK, :]
    totals = [jnp.zeros((8, 128), jnp.float32) for _ in chunks]
    for k in range(N_X):
        base = (x + k) % N_X * BLOCK
        for i in range(BLOCK // STEP):
            block = slice(i * STEP, (i + 1) * STEP)
            rows = pl.ds(pl.multiple_of(base + i * STEP, STEP), STEP)
            own, other = own_refs[k][block, :], other_refs[k][block, :]
            teacher, student = jnp.where(grp == 0, other, own), jnp.where(grp == 0, own, other)
            folded = jnp.zeros((STEP, 128), jnp.float32)
            for p in pairs:
                tokens = scratch_ref[p * 256 : (p + 1) * 256, :]
                values = exp_of(teacher, tokens, TEACHER_TEMP)
                tokens = jnp.concatenate(
                    [pack_refs[2 * p + h][OWN_ROWS:PACK, :] for h in range(2)], axis=0
                )
                others = exp_of(student, tokens, STUDENT_TEMP)
                for h in range(2):
                    n = 2 * p + h
                    half = values[:, h * 128 : (h + 1) * 128]
                    teacher_ref[places[n], rows, :] = half
                    folded += half
                    half = others[:, h * 128 : (h + 1) * 128]
                    student_ref[places[n], rows, :] = half
                    totals[n] += jnp.sum(half.reshape(STEP // 8, 8, 128), axis=0)
            column = jnp.sum(folded, axis=1, keepdims=True)
            for h in range(STEP // 128):
                line = pl.ds(base // 128 + i * (STEP // 128) + h, 1)
                sums = to_row(column[h * 128 : (h + 1) * 128])
                if resumed:
                    sums += sums_ref[line, :]
                    for target in range(N_COLGRP):
                        parts_ref[target, line, :] = sums
                else:
                    parts_ref[line, :] = sums
    for n, place in enumerate(places):
        total_ref[pl.ds(place, 1), :] = jnp.sum(totals[n], axis=0, keepdims=True)


def row_kernel(with_extra, *refs):
    if with_extra:
        parts_ref, exp_ref, extra_ref, out_ref, scale_ref = refs
    else:
        parts_ref, exp_ref, out_ref, scale_ref = refs
    scale = 1.0 / jnp.sum(parts_ref[...], axis=0)
    scale_ref[...] = scale
    totals = [jnp.zeros((8, 128), jnp.float32) for _ in range(N_Z)]
    for j in range(COLS // 128):
        column = to_column(scale[j : j + 1, :])
        for k in range(N_Z):
            weighted = exp_ref[k, j * 128 : (j + 1) * 128, :] * column
            totals[k] += jnp.sum(weighted.reshape(16, 8, 128), axis=0)
    mine = jnp.concatenate([jnp.sum(t, axis=0, keepdims=True) for t in totals], axis=0)
    if with_extra:
        mine = jnp.concatenate([mine, extra_ref[...].astype(jnp.float32)], axis=0)
    mine = mine.astype(jnp.bfloat16)
    for k in range(N_ROWGRP):
        out_ref[k] = mine


def col_kernel(with_weight, *refs):
    if with_weight:
        parts_ref, exp_ref, out_ref, weight_ref, vector_ref = refs
        for z in range(N_Z):
            weight_ref[z : z + 1, :] = parts_ref[z * N_Y].astype(jnp.float32)[8:9, :]
    else:
        parts_ref, exp_ref, out_ref, vector_ref = refs
    scale = 1.0 / jnp.sum(parts_ref[...].astype(jnp.float32), axis=0)[0:8, :]
    for j in range(COLS // 128):
        rows = slice(j * 128, (j + 1) * 128)
        folded = sum(exp_ref[k, rows, :] * scale[k : k + 1, :] for k in range(N_Z))
        vector_ref[j : j + 1, :] = to_row(jnp.sum(folded, axis=1, keepdims=True))
    for k in range(N_COLGRP):
        out_ref[k] = vector_ref[...]


def grad_kernel(
    other,
    pieces,
    place_ref,
    parts_ref,
    scale_ref,
    weight_ref,
    teacher_exp_ref,
    student_exp_ref,
    token_ref,
    out_ref,
):
    inverse = 1.0 / jnp.sum(parts_ref[...].astype(jnp.float32), axis=0)
    weight = weight_ref[...] * PROTOS
    teacher_row, student_row = inverse[0:8, :] * weight, inverse[8:16, :] * weight
    first = 1 - place_ref[0] if other else place_ref[0]
    for n, k in enumerate(pieces):
        base = (place_ref[1] + 2 * k + first) % N_X * BLOCK
        for i in range(BLOCK // 256):
            errors = []
            for h in range(2):
                start = base + i * 256 + h * 128
                column = to_column(scale_ref[pl.ds(start // 128, 1), :])
                rows = pl.ds(pl.multiple_of(start, 128), 128)
                line = []
                for z in range(N_Z):
                    targets = teacher_exp_ref[z, rows, :] * column * teacher_row[z : z + 1, :]
                    probs = student_exp_ref[z, rows, :] * student_row[z : z + 1, :]
                    line.append((probs - targets).astype(jnp.bfloat16))
                errors.append(jnp.concatenate(line, axis=1))
            out_ref[n, i * 256 : (i + 1) * 256, :] = jnp.dot(
                jnp.concatenate(errors, axis=0),
                token_ref[...],
                preferred_element_type=jnp.float32,
            ).astype(out_ref.dtype)


def call(kernel, outs, scratch, *args, flops=0, transcendentals=0, aliases=None):
    vmem = pl.BlockSpec(memory_space=pltpu.VMEM)
    smem = pl.BlockSpec(memory_space=pltpu.SMEM)
    return pl.pallas_call(
        kernel,
        out_shape=outs,
        in_specs=[smem if a.ndim == 1 else vmem for a in args],
        out_specs=[vmem] * len(outs),
        scratch_shapes=scratch,
        input_output_aliases=aliases or {},
        compiler_params=pltpu.CompilerParams(vmem_limit_bytes=VMEM_LIMIT),
        cost_estimate=pl.CostEstimate(
            flops=flops, transcendentals=transcendentals, bytes_accessed=COLS * ROWS * 4
        ),
    )(*args)


def shape(dims, dtype=jnp.float32):
    return jax.ShapeDtypeStruct(dims, dtype)


def per_device(features, masters, patch_mask):
    grp = lax.axis_index("grp")
    x = lax.axis_index("img") // N_Z * 2 + lax.axis_index("tp") // N_Y
    z = lax.axis_index("img") % N_Z
    place = jnp.stack([grp, x, z]).astype(jnp.int32)
    work = COLS * ROWS

    own_master = masters[0]
    other_master = swapped(own_master)
    other_features = swapped(features[0])
    pack, weight, unit, other_unit = unit_call(
        place,
        features[0],
        other_features,
        patch_mask.reshape(4, 128),
        own_master,
        other_master,
    )
    packs = {0: pack}
    for k in range(1, 5):
        packs[k] = from_z(packs[k - 1], 1)
        if k < 4:
            packs[N_Z - k] = from_z(packs[(N_Z - k + 1) % N_Z], -1)
    own_units = [unit, from_x(unit, 1), None, from_x(unit, -1)]
    own_units[2] = from_x(own_units[1], 1)
    near, _ = lax.optimization_barrier((tuple(own_units[1:]), (packs[3], packs[5])))
    other_units = [other_unit] + [swapped(block) for block in near]

    held = [
        shape((N_Z, COLS, 128)),
        shape((N_Z, COLS, 128)),
        shape((8, 128)),
        shape((ROWS, 256), jnp.bfloat16),
    ]

    def exponents(chunks, first_out, aliases, *carried):
        return call(
            functools.partial(exp_kernel, chunks, bool(carried)),
            [first_out] + held,
            [pltpu.VMEM((len(chunks) * OWN_ROWS, 256), jnp.bfloat16)],
            place,
            *(packs[k] for k in chunks),
            *own_units,
            *other_units,
            *carried,
            flops=len(chunks) * work * 256 // 2,
            transcendentals=len(chunks) * work // 4,
            aliases=aliases,
        )

    early, late = (0, 1, 7, 2, 6, 3), (5, 4)
    carried = exponents(early, shape((16, 128)), None)
    start = 1 + len(late) + 2 * N_X + 1
    col_parts, teacher_exp, student_exp, student_part, student_tokens = exponents(
        late,
        shape((N_COLGRP, 16, 128)),
        {start + n: 1 + n for n in range(4)},
        *carried,
    )

    for sweep in range(3):
        first, last = sweep == 0, sweep == 2
        extra = (weight,) if first else (student_part,) if last else ()
        col_parts = exchange(col_parts, COL_GROUPS)
        row_parts, col_scale = call(
            functools.partial(row_kernel, first or last),
            [shape((N_ROWGRP, 16 if extra else 8, 128), jnp.bfloat16), shape((16, 128))],
            [],
            col_parts,
            teacher_exp,
            *extra,
            flops=2 * work,
        )
        row_parts = exchange(row_parts, ROW_GROUPS)
        if not last:
            col_parts, *rest = call(
                functools.partial(col_kernel, first),
                [shape((N_COLGRP, 16, 128))] + [shape((8, 128))] * first,
                [pltpu.VMEM((16, 128), jnp.float32)],
                row_parts,
                teacher_exp,
                flops=2 * work,
            )
            if first:
                (weights,) = rest

    def partial_gradient(other, pieces, dtype):
        (out,) = call(
            functools.partial(grad_kernel, other, pieces),
            [shape((len(pieces), BLOCK, 256), dtype)],
            [],
            place,
            row_parts,
            col_scale,
            weights,
            teacher_exp,
            student_exp,
            student_tokens,
            flops=work * 256,
        )
        return out

    received = swapped(partial_gradient(True, (0, 1), jnp.bfloat16))
    chip = partial_gradient(False, (0, 1), jnp.float32) + received.astype(jnp.float32)
    near, far = chip[0].astype(jnp.bfloat16), chip[1].astype(jnp.bfloat16)

    def sent(block, source, distance):
        return permuted(
            block,
            lambda grp, x, y, z: (0, (x + distance) % N_X, y, z) if grp == source else None,
        ).astype(jnp.float32)

    gradient = chip[0] + sent(far, 0, 2) + sent(near, 1, 1) + sent(far, 1, 3)
    blended = MOMENTUM * own_master + (1.0 - MOMENTUM) * other_master
    return jnp.where(grp == 1, blended, gradient)[None]


def solution(mesh):
    in_specs = (P("grp", "img", None), P("grp", ("img", "tp"), None), P("img"))
    out_specs = P("grp", ("img", "tp"), None)
    return jax.shard_map(
        per_device, mesh=mesh, in_specs=in_specs, out_specs=out_specs, check_vma=False
    )
```

```python
import functools

import jax
import jax.numpy as jnp
from jax import lax
from jax.experimental import pallas as pl
from jax.experimental.pallas import tpu as pltpu
from jax.sharding import PartitionSpec as P

PROTOS = 65536
PATCHES = 256
MOMENTUM = 0.994
TEACHER_TEMP = 0.07
STUDENT_TEMP = 0.1
EPS = 1e-06
LOG2E = 1.4426950408889634

AXES = ("grp", "img", "tp")
N_GRP, N_IMG, N_TP = 2, 16, 8
N_X, N_Y, N_Z = 4, 4, 8
BLOCK = 512
HALF = 256
STEP = 512
OWN_ROWS = 128
PACK = 2 * OWN_ROWS
ROWS = N_Z * OWN_ROWS
COLS = N_X * BLOCK
N_ROWGRP = N_Y * N_Z
N_COLGRP = N_GRP * N_X
VMEM_LIMIT = 16 * 1024 * 1024


def coordinates(device):
    grp, rest = divmod(device, N_IMG * N_TP)
    img, tp = divmod(rest, N_TP)
    x_hi, z = divmod(img, N_Z)
    x_lo, y = divmod(tp, N_Y)
    return grp, x_hi * 2 + x_lo, y, z


def device_at(grp, x, y, z):
    return ((grp * 2 + x // 2) * N_Z + z) * N_TP + x % 2 * N_Y + y


def groups_of(key):
    found = {}
    for device in range(N_GRP * N_IMG * N_TP):
        found.setdefault(key(*coordinates(device)), []).append(device)
    return list(found.values())


COL_GROUPS = groups_of(lambda grp, x, y, z: (y, z))
ROW_GROUPS = groups_of(lambda grp, x, y, z: (grp, x))


def exchange(blocks, groups):
    return lax.all_to_all(blocks, AXES, 0, 0, axis_index_groups=groups, tiled=True)


def swapped(block):
    return lax.ppermute(block, "grp", [(0, 1), (1, 0)])


def permuted(block, target_of):
    route = []
    for device in range(N_GRP * N_IMG * N_TP):
        target = target_of(*coordinates(device))
        if target is not None:
            route.append((device, device_at(*target)))
    return lax.ppermute(block, AXES, route)


def from_x(block, distance):
    return permuted(block, lambda grp, x, y, z: (grp, (x - distance) % N_X, y, z))


def from_z(block, distance):
    return permuted(block, lambda grp, x, y, z: (grp, x, y, (z - distance) % N_Z))


def unit_rows(values):
    return (values / jnp.sqrt(jnp.sum(values * values, -1, keepdims=True) + EPS)).astype(
        jnp.bfloat16
    )


def diagonal():
    return lax.broadcasted_iota(jnp.int32, (128, 128), 0) == lax.broadcasted_iota(
        jnp.int32, (128, 128), 1
    )


def to_row(column):
    return jnp.sum(jnp.where(diagonal(), column, 0.0), axis=0, keepdims=True)


def to_column(row):
    return jnp.sum(jnp.where(diagonal(), row, 0.0), axis=1, keepdims=True)


def lanes(pieces):
    return jnp.concatenate([pieces[k : k + 1, :] for k in range(pieces.shape[0])], axis=1)


def pieces_of(row):
    return jnp.concatenate([row[:, k * 128 : (k + 1) * 128] for k in range(8)], axis=0)


def unit_kernel(
    place_ref,
    features_ref,
    other_features_ref,
    mask_ref,
    own_ref,
    other_ref,
    pack_ref,
    weight_ref,
    unit_ref,
    other_unit_ref,
):
    grp, x = place_ref[0], place_ref[1]

    @pl.when(pl.program_id(0) == 0)
    def _():
        own = unit_rows(features_ref[...].astype(jnp.float32))
        other = unit_rows(other_features_ref[...].astype(jnp.float32))
        teacher = jnp.where(grp == 0, other, own)
        student = jnp.where(grp == 0, own, other)
        crop = mask_ref[pl.ds(x % 2 * 2, 2), :].astype(jnp.float32)
        count = jnp.maximum(jnp.sum(crop), 1.0)
        weight = mask_ref[pl.ds(x % 2 * 2 + grp, 1), :].astype(jnp.float32)
        weight = weight / (STUDENT_TEMP * count)
        weight_ref[...] = jnp.broadcast_to(weight, (8, 128)).astype(jnp.bfloat16)
        pack_ref[0:OWN_ROWS, :] = teacher
        pack_ref[OWN_ROWS:PACK, :] = student

    own, other = own_ref[...], other_ref[...]
    student = jnp.where(grp == 0, own, other)
    blended = MOMENTUM * jnp.where(grp == 0, other, own) + (1.0 - MOMENTUM) * student
    student, blended = unit_rows(student), unit_rows(blended)
    unit_ref[...] = jnp.where(grp == 0, student, blended)
    other_unit_ref[...] = jnp.where(grp == 0, blended, student)


def in_hbm(array):
    return pltpu.with_memory_space_constraint(array, pltpu.HBM)


def unit_call(place, features, other_features, mask, own_master, other_master):
    rows = BLOCK
    picked = pl.BlockSpec((OWN_ROWS, 256), lambda i, place: (place[1] % 2 * 2 + place[0], 0))
    part = pl.BlockSpec((rows, 256), lambda i, place: (i, 0))
    return pl.pallas_call(
        unit_kernel,
        out_shape=[
            shape((PACK, 256), jnp.bfloat16),
            shape((8, 128), jnp.bfloat16),
            shape((BLOCK, 256), jnp.bfloat16),
            shape((BLOCK, 256), jnp.bfloat16),
        ],
        grid_spec=pltpu.PrefetchScalarGridSpec(
            num_scalar_prefetch=1,
            grid=(1,),
            in_specs=[
                picked,
                picked,
                pl.BlockSpec((4, 128), lambda i, place: (0, 0)),
                part,
                part,
            ],
            out_specs=[
                pl.BlockSpec((PACK, 256), lambda i, place: (0, 0)),
                pl.BlockSpec((8, 128), lambda i, place: (0, 0)),
                part,
                part,
            ],
        ),
        compiler_params=pltpu.CompilerParams(vmem_limit_bytes=VMEM_LIMIT),
    )(place, in_hbm(features), other_features, in_hbm(mask), in_hbm(own_master), other_master)


def exp_of(protos, tokens, temperature):
    logits = lax.dot_general(
        protos, tokens, (((1,), (1,)), ((), ())), preferred_element_type=jnp.float32
    )
    return jnp.exp2(logits * (LOG2E / temperature))


def exp_kernel(chunks, resumed, *refs):
    place_ref, pack_refs = refs[0], refs[1 : 1 + len(chunks)]
    refs = refs[1 + len(chunks) :]
    own_refs, other_refs, refs = refs[0:4], refs[4:8], refs[8:]
    if resumed:
        sums_ref, refs = refs[0], refs[5:]
    parts_ref, teacher_ref, student_ref, total_ref, token_ref, scratch_ref = refs
    grp, x, z = place_ref[0], place_ref[1], place_ref[2]
    places = [(z + k) % N_Z for k in chunks]
    pairs = range(len(chunks) // 2)
    for n, place in enumerate(places):
        scratch_ref[n * OWN_ROWS : (n + 1) * OWN_ROWS, :] = pack_refs[n][0:OWN_ROWS, :]
        rows = pl.ds(pl.multiple_of(place * OWN_ROWS, OWN_ROWS), OWN_ROWS)
        token_ref[rows, :] = pack_refs[n][OWN_ROWS:PACK, :]
    totals = [jnp.zeros((8, 128), jnp.float32) for _ in chunks]
    for k in range(N_X):
        base = (x + k) % N_X * BLOCK
        for i in range(BLOCK // STEP):
            block = slice(i * STEP, (i + 1) * STEP)
            rows = pl.ds(pl.multiple_of(base + i * STEP, STEP), STEP)
            own, other = own_refs[k][block, :], other_refs[k][block, :]
            teacher, student = jnp.where(grp == 0, other, own), jnp.where(grp == 0, own, other)
            folded = jnp.zeros((STEP, 128), jnp.float32)
            for p in pairs:
                tokens = scratch_ref[p * 256 : (p + 1) * 256, :]
                values = exp_of(teacher, tokens, TEACHER_TEMP)
                tokens = jnp.concatenate(
                    [pack_refs[2 * p + h][OWN_ROWS:PACK, :] for h in range(2)], axis=0
                )
                others = exp_of(student, tokens, STUDENT_TEMP)
                for h in range(2):
                    n = 2 * p + h
                    half = values[:, h * 128 : (h + 1) * 128]
                    teacher_ref[places[n], rows, :] = half
                    folded += half
                    half = others[:, h * 128 : (h + 1) * 128]
                    student_ref[places[n], rows, :] = half
                    totals[n] += jnp.sum(half.reshape(STEP // 8, 8, 128), axis=0)
            column = jnp.sum(folded, axis=1, keepdims=True)
            for h in range(STEP // 128):
                line = pl.ds(base // 128 + i * (STEP // 128) + h, 1)
                sums = to_row(column[h * 128 : (h + 1) * 128])
                if resumed:
                    sums += sums_ref[line, :]
                    for target in range(N_COLGRP):
                        parts_ref[target, line, :] = sums
                else:
                    parts_ref[line, :] = sums
    for n, place in enumerate(places):
        total_ref[pl.ds(place, 1), :] = jnp.sum(totals[n], axis=0, keepdims=True)


def row_kernel(with_extra, *refs):
    if with_extra:
        parts_ref, exp_ref, extra_ref, out_ref, scale_ref = refs
    else:
        parts_ref, exp_ref, out_ref, scale_ref = refs
    scale = 1.0 / jnp.sum(parts_ref[...].astype(jnp.float32), axis=0)
    scale_ref[...] = scale
    totals = [jnp.zeros((8, 128), jnp.float32) for _ in range(N_Z)]
    for j in range(COLS // 128):
        column = to_column(scale[j : j + 1, :])
        for k in range(N_Z):
            weighted = exp_ref[k, j * 128 : (j + 1) * 128, :] * column
            totals[k] += jnp.sum(weighted.reshape(16, 8, 128), axis=0)
    mine = jnp.concatenate([jnp.sum(t, axis=0, keepdims=True) for t in totals], axis=0)
    if with_extra:
        mine = jnp.concatenate([mine, extra_ref[...].astype(jnp.float32)], axis=0)
    mine = mine.astype(jnp.bfloat16)
    for k in range(N_ROWGRP):
        out_ref[k] = mine


def col_kernel(with_weight, *refs):
    if with_weight:
        parts_ref, exp_ref, out_ref, weight_ref, vector_ref = refs
        for z in range(N_Z):
            weight_ref[z : z + 1, :] = parts_ref[z * N_Y].astype(jnp.float32)[8:9, :]
    else:
        parts_ref, exp_ref, out_ref, vector_ref = refs
    scale = 1.0 / jnp.sum(parts_ref[...].astype(jnp.float32), axis=0)[0:8, :]
    for j in range(COLS // 128):
        rows = slice(j * 128, (j + 1) * 128)
        folded = sum(exp_ref[k, rows, :] * scale[k : k + 1, :] for k in range(N_Z))
        vector_ref[j : j + 1, :] = to_row(jnp.sum(folded, axis=1, keepdims=True))
    for k in range(N_COLGRP):
        out_ref[k] = vector_ref[...].astype(jnp.bfloat16)


def grad_kernel(
    other,
    pieces,
    place_ref,
    parts_ref,
    scale_ref,
    weight_ref,
    teacher_exp_ref,
    student_exp_ref,
    token_ref,
    out_ref,
):
    inverse = 1.0 / jnp.sum(parts_ref[...].astype(jnp.float32), axis=0)
    weight = weight_ref[...] * PROTOS
    teacher_row, student_row = inverse[0:8, :] * weight, inverse[8:16, :] * weight
    first = 1 - place_ref[0] if other else place_ref[0]
    for n, k in enumerate(pieces):
        base = (place_ref[1] + 2 * k + first) % N_X * BLOCK
        for i in range(BLOCK // 256):
            errors = []
            for h in range(2):
                start = base + i * 256 + h * 128
                column = to_column(scale_ref[pl.ds(start // 128, 1), :])
                rows = pl.ds(pl.multiple_of(start, 128), 128)
                line = []
                for z in range(N_Z):
                    targets = teacher_exp_ref[z, rows, :] * column * teacher_row[z : z + 1, :]
                    probs = student_exp_ref[z, rows, :] * student_row[z : z + 1, :]
                    line.append((probs - targets).astype(jnp.bfloat16))
                errors.append(jnp.concatenate(line, axis=1))
            out_ref[n, i * 256 : (i + 1) * 256, :] = jnp.dot(
                jnp.concatenate(errors, axis=0),
                token_ref[...],
                preferred_element_type=jnp.float32,
            ).astype(out_ref.dtype)


def call(kernel, outs, scratch, *args, flops=0, transcendentals=0, aliases=None):
    vmem = pl.BlockSpec(memory_space=pltpu.VMEM)
    smem = pl.BlockSpec(memory_space=pltpu.SMEM)
    return pl.pallas_call(
        kernel,
        out_shape=outs,
        in_specs=[smem if a.ndim == 1 else vmem for a in args],
        out_specs=[vmem] * len(outs),
        scratch_shapes=scratch,
        input_output_aliases=aliases or {},
        compiler_params=pltpu.CompilerParams(vmem_limit_bytes=VMEM_LIMIT),
        cost_estimate=pl.CostEstimate(
            flops=flops, transcendentals=transcendentals, bytes_accessed=COLS * ROWS * 4
        ),
    )(*args)


def shape(dims, dtype=jnp.float32):
    return jax.ShapeDtypeStruct(dims, dtype)


def per_device(features, masters, patch_mask):
    grp = lax.axis_index("grp")
    x = lax.axis_index("img") // N_Z * 2 + lax.axis_index("tp") // N_Y
    z = lax.axis_index("img") % N_Z
    place = jnp.stack([grp, x, z]).astype(jnp.int32)
    work = COLS * ROWS

    own_master = masters[0]
    other_master = swapped(own_master)
    other_features = swapped(features[0])
    pack, weight, unit, other_unit = unit_call(
        place,
        features[0],
        other_features,
        patch_mask.reshape(4, 128),
        own_master,
        other_master,
    )
    packs = {0: pack}
    for k in range(1, 5):
        packs[k] = from_z(packs[k - 1], 1)
        if k < 4:
            packs[N_Z - k] = from_z(packs[(N_Z - k + 1) % N_Z], -1)
    own_units = [unit, from_x(unit, 1), None, from_x(unit, -1)]
    own_units[2] = from_x(own_units[1], 1)
    near, _ = lax.optimization_barrier((tuple(own_units[1:]), (packs[3], packs[5])))
    other_units = [other_unit] + [swapped(block) for block in near]

    held = [
        shape((N_Z, COLS, 128)),
        shape((N_Z, COLS, 128)),
        shape((8, 128)),
        shape((ROWS, 256), jnp.bfloat16),
    ]

    def exponents(chunks, first_out, aliases, *carried):
        return call(
            functools.partial(exp_kernel, chunks, bool(carried)),
            [first_out] + held,
            [pltpu.VMEM((len(chunks) * OWN_ROWS, 256), jnp.bfloat16)],
            place,
            *(packs[k] for k in chunks),
            *own_units,
            *other_units,
            *carried,
            flops=len(chunks) * work * 256 // 2,
            transcendentals=len(chunks) * work // 4,
            aliases=aliases,
        )

    early, late = (0, 1, 7, 2, 6, 3), (5, 4)
    carried = exponents(early, shape((16, 128)), None)
    start = 1 + len(late) + 2 * N_X + 1
    col_parts, teacher_exp, student_exp, student_part, student_tokens = exponents(
        late,
        shape((N_COLGRP, 16, 128)),
        {start + n: 1 + n for n in range(4)},
        *carried,
    )

    for sweep in range(3):
        first, last = sweep == 0, sweep == 2
        extra = (weight,) if first else (student_part,) if last else ()
        col_parts = exchange(col_parts, COL_GROUPS)
        row_parts, col_scale = call(
            functools.partial(row_kernel, first or last),
            [shape((N_ROWGRP, 16 if extra else 8, 128), jnp.bfloat16), shape((16, 128))],
            [],
            col_parts,
            teacher_exp,
            *extra,
            flops=2 * work,
        )
        row_parts = exchange(row_parts, ROW_GROUPS)
        if not last:
            col_parts, *rest = call(
                functools.partial(col_kernel, first),
                [shape((N_COLGRP, 16, 128), jnp.bfloat16)] + [shape((8, 128))] * first,
                [pltpu.VMEM((16, 128), jnp.float32)],
                row_parts,
                teacher_exp,
                flops=2 * work,
            )
            if first:
                (weights,) = rest

    def partial_gradient(other, pieces, dtype):
        (out,) = call(
            functools.partial(grad_kernel, other, pieces),
            [shape((len(pieces), BLOCK, 256), dtype)],
            [],
            place,
            row_parts,
            col_scale,
            weights,
            teacher_exp,
            student_exp,
            student_tokens,
            flops=work * 256,
        )
        return out

    received = swapped(partial_gradient(True, (0, 1), jnp.bfloat16))
    chip = partial_gradient(False, (0, 1), jnp.float32) + received.astype(jnp.float32)
    near, far = chip[0].astype(jnp.bfloat16), chip[1].astype(jnp.bfloat16)

    def sent(block, source, distance):
        return permuted(
            block,
            lambda grp, x, y, z: (0, (x + distance) % N_X, y, z) if grp == source else None,
        ).astype(jnp.float32)

    gradient = chip[0] + sent(far, 0, 2) + sent(near, 1, 1) + sent(far, 1, 3)
    blended = MOMENTUM * own_master + (1.0 - MOMENTUM) * other_master
    return jnp.where(grp == 1, blended, gradient)[None]


def solution(mesh):
    in_specs = (P("grp", "img", None), P("grp", ("img", "tp"), None), P("img"))
    out_specs = P("grp", ("img", "tp"), None)
    return jax.shard_map(
        per_device, mesh=mesh, in_specs=in_specs, out_specs=out_specs, check_vma=False
    )
```
